128 devices in a mesh: wide: 16 (over y, x_hi, core), narrow: 8 (over z, x_lo).
Axes of the slice: x: 4 (x_hi: 2, x_lo: 2; x = x_hi * 2 + x_lo), y: 4, z: 4, core: 2. Of those that a mesh axis runs over, the one named last changes fastest.
Arguments:
- features: bfloat16 [524288, 512], P(('wide', 'narrow')), may hold values from -6 to 6
- adjacency: bfloat16 [12288, 128, 128], P(('wide', 'narrow')), may hold values from -0.375 to 0.375
- block_rows: int32 [128, 96], P(('wide', 'narrow')), may hold values from 0 to 31, as said below
- block_cols: int32 [128, 96], P(('wide', 'narrow')), may hold values from 0 to 39, as said below
- block_count: int32 [128], P(('wide', 'narrow')), may hold values from 40 to 96, as said below
- node_count: int32 [128], P(('wide', 'narrow')), may hold values from 2048 to 4096, as said below
- halo_index: int32 [128, 4, 256], P(('wide', 'narrow')), may hold values from 0 to 2047, as said below
- weight: bfloat16 [512, 512], replicated, may hold values from -0.25 to 0.25
- bias: float32 [512], replicated, may hold values from -3 to 3
- out_grad: bfloat16 [524288, 512], P(('wide', 'narrow')), may hold values from -6 to 6
Outputs:
- output: bfloat16 [524288, 512], P(('wide', 'narrow'))
- input_grad: bfloat16 [524288, 512], P(('wide', 'narrow'))
- weight_grad: float32 [512, 512], replicated
- bias_grad: float32 [512], replicated
The draws below stay inside these ranges and needn't reach their ends.
Inputs may be any that keep to these rules, and one draw needn't show every extreme that they name: `block_count`: each device's live slots include every one of its 32 diagonal blocks and every one of its 8 halo column blocks at least once; some device has all 96 slots live. `block_rows`: within range for live and non-live slots. `block_cols`: within range for live and non-live slots. `node_count`: some device has all 4096 slots live. `halo_index`: the 1024 rows of one device are distinct and all live.
All inputs are finite; a program needn't handle non-finite values.
Results may differ from the reference program's by a relative error of at most 0.0062.
Values may be sent and summed in bfloat16 or wider, within the bound.
No kernel may reach another device: no remote copies, remote signals or barrier semaphores. Data moves between devices by JAX's collectives and lax.ppermute only.
A program may use at most 192 MiB of HBM per device.

```python
import math
import jax
import jax.numpy as jnp
from jax import lax

F = 512
BS = 128
NODE_DEV = 4096
HALO = 256
RB = 32
ECB = 40
BLK = 96
TOTAL = 524288
N_WIDE = 16
N_NARROW = 8
DEVICES = 128


def layout_tables(key):
    key_count = jax.random.fold_in(key, 11)
    key_hot = jax.random.fold_in(key, 12)
    key_cold = jax.random.fold_in(key, 13)
    key_rows = jax.random.fold_in(key, 14)
    key_extra = jax.random.fold_in(key, 15)
    key_perm = jax.random.fold_in(key, 16)
    spare = BLK - ECB
    draws = jax.random.randint(key_count, (DEVICES,), 0, spare + 1)
    count = ECB + draws * draws // max(spare, 1)
    hot = jax.random.randint(key_hot, (), 0, DEVICES)
    cold = (hot + 1 + jax.random.randint(key_cold, (), 0, DEVICES - 1)) % DEVICES
    count = count.at[hot].set(BLK).at[cold].set(ECB)
    halo_rowsel = jax.random.randint(key_rows, (DEVICES, ECB - RB), 0, RB)
    fixed_rows = jnp.concatenate([jnp.broadcast_to(jnp.arange(RB, dtype=jnp.int32), (DEVICES, RB)), halo_rowsel.astype(jnp.int32)], 1)
    fixed_cols = jnp.broadcast_to(jnp.arange(ECB, dtype=jnp.int32), (DEVICES, ECB))
    perm_keys = jax.random.split(key_perm, DEVICES)
    perms = jax.vmap(lambda k: jax.random.permutation(k, ECB))(perm_keys)
    fixed_rows = jnp.take_along_axis(fixed_rows, perms, 1)
    fixed_cols = jnp.take_along_axis(fixed_cols, perms, 1)
    extra_rows = jax.random.randint(jax.random.fold_in(key_extra, 1), (DEVICES, spare), 0, RB)
    extra_cols = jax.random.randint(jax.random.fold_in(key_extra, 2), (DEVICES, spare), 0, ECB)
    rows = jnp.concatenate([fixed_rows, extra_rows.astype(jnp.int32)], 1)
    cols = jnp.concatenate([fixed_cols, extra_cols.astype(jnp.int32)], 1)
    return (rows, cols, count.astype(jnp.int32))


def draw_block_rows(key, part):
    return layout_tables(key)[0]


def draw_block_cols(key, part):
    return layout_tables(key)[1]


def draw_block_count(key, part):
    return layout_tables(key)[2]


def draw_node_count(key, part):
    counts = jax.random.randint(jax.random.fold_in(key, 21), (DEVICES,), NODE_DEV // 2, NODE_DEV + 1)
    full = jax.random.randint(jax.random.fold_in(key, 22), (), 0, DEVICES)
    return counts.at[full].set(NODE_DEV).astype(jnp.int32)


def draw_halo_index(key, part):
    keys = jax.random.split(jax.random.fold_in(key, 31), DEVICES)
    picks = jax.vmap(lambda k: jax.random.permutation(k, NODE_DEV // 2)[:4 * HALO])(keys)
    return picks.reshape(DEVICES, 4, HALO).astype(jnp.int32)


def levels(own_key, shape, shards, low, largest):
    def one(axis_at, blocks):
        steps = jax.random.uniform(jax.random.fold_in(jax.random.fold_in(own_key, 6), axis_at), (blocks,), jnp.float32, low / len(shards), largest / len(shards))
        return jnp.repeat(jnp.exp(steps), shape[axis_at] // blocks).reshape((-1,) + (1,) * (len(shape) - axis_at - 1))

    loudness = one(*shards[0])
    for cut in shards[1:]:
        loudness = loudness * one(*cut)
    return loudness


def centred(stream_key, dims, width, bound, pieces=(), kind=jnp.bfloat16):
    values = jax.random.normal(stream_key, dims, jnp.float32) * width
    if len(pieces) > 0:
        values = levels(stream_key, dims, pieces, -0.22, 0.18) * values
    return jnp.clip(values, min=-bound, max=bound).astype(kind)


def setup_inputs(seed: int = 0) -> dict:
    seeds = jax.random.split(jax.random.key(seed), 11)
    features = centred(seeds[0], (TOTAL, F), 1.0, 6.0, ((0, 128),))
    adjacency = centred(seeds[1], (DEVICES * BLK, BS, BS), (2 * BS) ** -0.5, 0.375, ((0, 128),))
    block_rows = draw_block_rows(jax.random.fold_in(seeds[10], 71), 0)
    block_cols = draw_block_cols(jax.random.fold_in(seeds[10], 71), 0)
    block_count = draw_block_count(jax.random.fold_in(seeds[10], 71), 0)
    node_count = draw_node_count(jax.random.fold_in(seeds[10], 71), 0)
    halo_index = draw_halo_index(jax.random.fold_in(seeds[10], 71), 0)
    weight = centred(seeds[7], (F, F), F ** -0.5, 0.25)
    bias = centred(seeds[8], (F,), 0.5, 3.0, (), jnp.float32)
    out_grad = centred(seeds[9], (TOTAL, F), 1.0, 6.0, ((0, 128),))
    return {"features": features, "adjacency": adjacency, "block_rows": block_rows, "block_cols": block_cols, "block_count": block_count, "node_count": node_count, "halo_index": halo_index, "weight": weight, "bias": bias, "out_grad": out_grad}


def device_pass(items, weight, bias):
    own, halos, blocks, rows, cols, count, keep, grads = items
    extended = jnp.concatenate([own, halos], 0).reshape(ECB, BS, F)
    live = jnp.arange(BLK) < count

    def forward_step(total, item):
        tile, row_id, col_id, alive = item
        prod = jnp.dot(tile, extended[col_id], preferred_element_type=jnp.float32)
        return (total.at[row_id].add(jnp.where(alive, prod, jnp.float32(0.0))), None)
    summed, _ = lax.scan(forward_step, jnp.zeros((RB, BS, F), jnp.float32), (blocks, rows, cols, live))
    aggregated = summed.reshape(NODE_DEV, F).astype(jnp.bfloat16)
    pre = jnp.dot(aggregated, weight, preferred_element_type=jnp.float32) + bias
    sig = jax.nn.sigmoid(pre)
    output = jnp.where(keep[:, None], pre * sig, jnp.float32(0.0)).astype(jnp.bfloat16)
    dpre = jnp.where(keep[:, None], grads.astype(jnp.float32) * sig * (1.0 + pre * (1.0 - sig)), jnp.float32(0.0)).astype(jnp.bfloat16)
    weight_part = jnp.dot(aggregated.T, dpre, preferred_element_type=jnp.float32)
    bias_part = lax.optimization_barrier(jnp.sum(dpre.astype(jnp.float32), 0))
    back = jnp.dot(dpre, weight.T, preferred_element_type=jnp.float32).astype(jnp.bfloat16).reshape(RB, BS, F)

    def backward_step(total, item):
        tile, row_id, col_id, alive = item
        prod = jnp.dot(tile.T, back[row_id], preferred_element_type=jnp.float32)
        return (total.at[col_id].add(jnp.where(alive, prod, jnp.float32(0.0))), None)
    spread, _ = lax.scan(backward_step, jnp.zeros((ECB, BS, F), jnp.float32), (blocks, rows, cols, live))
    own_part = spread[:RB].reshape(NODE_DEV, F)
    halo_part = spread[RB:].reshape(4, HALO, F).astype(jnp.bfloat16)
    return (output, weight_part, bias_part, own_part, halo_part)

def reference(features, adjacency, block_rows, block_cols, block_count, node_count, halo_index, weight, bias, out_grad):
    n_wide = N_WIDE
    n_narrow = N_NARROW
    feats = features.reshape(DEVICES, NODE_DEV, F)
    keep = jnp.arange(NODE_DEV)[None, :] < node_count[:, None]
    masked = jnp.where(keep[:, :, None], feats, jnp.zeros_like(feats))
    packed = jax.vmap(lambda rows_of, picks: rows_of[picks])(masked, halo_index)
    grid = packed.reshape(n_wide, n_narrow, 4, HALO, F)
    zero_wide = jnp.zeros((1, n_narrow, HALO, F), jnp.bfloat16)
    zero_narrow = jnp.zeros((n_wide, 1, HALO, F), jnp.bfloat16)
    seg_a = jnp.concatenate([zero_wide, grid[:-1, :, 1]], 0)
    seg_b = jnp.concatenate([grid[1:, :, 0], zero_wide], 0)
    seg_c = jnp.concatenate([zero_narrow, grid[:, :-1, 3]], 1)
    seg_d = jnp.concatenate([grid[:, 1:, 2], zero_narrow], 1)
    halos = jnp.stack([seg_a, seg_b, seg_c, seg_d], 2).reshape(DEVICES, 4 * HALO, F)
    blocks = adjacency.reshape(DEVICES, BLK, BS, BS)
    grads = out_grad.reshape(DEVICES, NODE_DEV, F)
    output, weight_parts, bias_parts, own_part, halo_part = lax.map(lambda items: device_pass(items, weight, bias), (masked, halos, blocks, block_rows, block_cols, block_count, keep, grads))
    scale = 1.0 / math.sqrt(TOTAL)
    weight_grad = lax.optimization_barrier(jnp.sum(weight_parts, 0)) * scale
    bias_grad = lax.optimization_barrier(jnp.sum(bias_parts, 0)) * scale
    hgrid = halo_part.astype(jnp.float32).reshape(n_wide, n_narrow, 4, HALO, F)
    fzero_wide = jnp.zeros((1, n_narrow, HALO, F), jnp.float32)
    fzero_narrow = jnp.zeros((n_wide, 1, HALO, F), jnp.float32)
    in_a = jnp.concatenate([fzero_wide, hgrid[:-1, :, 1]], 0)
    in_b = jnp.concatenate([hgrid[1:, :, 0], fzero_wide], 0)
    in_c = jnp.concatenate([fzero_narrow, hgrid[:, :-1, 3]], 1)
    in_d = jnp.concatenate([hgrid[:, 1:, 2], fzero_narrow], 1)
    incoming = jnp.stack([in_a, in_b, in_c, in_d], 2).reshape(DEVICES, 4 * HALO, F)
    summed = jax.vmap(lambda base, picks, extra: base.at[picks].add(extra))(own_part, halo_index.reshape(DEVICES, 4 * HALO), incoming)
    input_grad = jnp.where(keep[:, :, None], summed, jnp.float32(0.0)).astype(jnp.bfloat16)
    return (output.reshape(TOTAL, F), input_grad.reshape(TOTAL, F), weight_grad, bias_grad)
```

```python
import math

import jax
import jax.numpy as jnp
from jax import lax
from jax.experimental import pallas as pl
from jax.experimental.pallas import tpu as pltpu
from jax.sharding import PartitionSpec as P

F = 512
BS = 128
NODES = 4096
HALO = 256
RB = 32
ECB = 40
BLK = 96
HALF = 2048
CHUNK = 512
PEERS = 128
UNROLL = 4
BF = jnp.bfloat16
F32 = jnp.float32
VMEM_BYTES = 56 * 1024 * 1024
AXES = ("wide", "narrow")


def pack_kernel(picks, feats, out0, out1, out2, out3):
    outs = (out0, out1, out2, out3)
    lane = lax.broadcasted_iota(jnp.int32, (BS, BS), 1)
    for k in range(4):
        parts = []
        for h in range(2):
            row = picks[k : k + 1, h * BS : (h + 1) * BS]
            parts.append(jnp.transpose(jnp.broadcast_to(row.astype(F32), (BS, BS))).astype(jnp.int32))
        onehot = jnp.concatenate(
            [
                jnp.concatenate([jnp.where(t == lane + c * BS, F32(1.0), F32(0.0)).astype(BF) for c in range(HALF // BS)], 1)
                for t in parts
            ],
            0,
        )
        outs[k][...] = jnp.dot(onehot, feats[...], preferred_element_type=F32).astype(BF)


def pack(picks, features):
    return pl.pallas_call(
        pack_kernel,
        grid=(1,),
        in_specs=[
            pl.BlockSpec((4, HALO), lambda i: (0, 0)),
            pl.BlockSpec((HALF, F), lambda i: (0, 0)),
        ],
        out_specs=[pl.BlockSpec((HALO, F), lambda i: (0, 0))] * 4,
        out_shape=[jax.ShapeDtypeStruct((HALO, F), BF)] * 4,
        compiler_params=pltpu.CompilerParams(vmem_limit_bytes=VMEM_BYTES),
        name="pack",
    )(picks, features)


def main_kernel(
    rows,
    cols,
    count,
    nodes,
    feats,
    adj_in,
    h0,
    h1,
    h2,
    h3,
    weight_in,
    bias,
    grads_in,
    output,
    input_grad,
    own,
    ret0,
    ret1,
    ret2,
    ret3,
    terms,
    ext,
    adj,
    acc,
    spread,
    weight,
    grads,
    outbuf,
    back,
    wacc,
    bacc,
    sems,
    osems,
):
    live = count[0]
    alive = nodes[0]
    loads = [
        pltpu.make_async_copy(adj_in, adj, sems.at[0]),
        pltpu.make_async_copy(feats, ext.at[pl.ds(0, NODES)], sems.at[1]),
    ]
    for k, h in enumerate((h0, h1, h2, h3)):
        loads.append(pltpu.make_async_copy(h, ext.at[pl.ds(NODES + k * HALO, HALO)], sems.at[2 + k]))
    late = [
        pltpu.make_async_copy(weight_in, weight, sems.at[6]),
        pltpu.make_async_copy(grads_in, grads, sems.at[7]),
    ]
    for c in loads + late:
        c.start()

    @pl.loop(0, RB + 1)
    def _(r):
        acc[pl.ds(pl.multiple_of(r * BS, BS), BS), :] = jnp.zeros((BS, F), F32)

    @pl.loop(0, ECB + 1)
    def _(r):
        spread[pl.ds(pl.multiple_of(r * BS, BS), BS), :] = jnp.zeros((BS, F), F32)

    wacc[...] = jnp.zeros_like(wacc)
    bacc[...] = jnp.zeros_like(bacc)
    for c in loads:
        c.wait()

    @pl.loop(alive // BS, RB)
    def _(r):
        at = pl.ds(pl.multiple_of(r * BS, BS), BS)
        line = lax.broadcasted_iota(jnp.int32, (BS, F), 0) + r * BS
        ext[at, :] = jnp.where(line < alive, ext[at, :].astype(F32), F32(0.0)).astype(BF)

    def block(ref, i):
        return ref[pl.ds(pl.multiple_of(i * BS, BS), BS), :]

    @pl.loop(0, BLK // UNROLL)
    def _(i):
        prods, targets = [], []
        for u in range(UNROLL):
            b = i * UNROLL + u
            prods.append(jnp.dot(adj[b], block(ext, cols[0, b]), preferred_element_type=F32))
            targets.append(jnp.where(b < live, rows[0, b], RB))
        for prod, r in zip(prods, targets):
            at = pl.ds(pl.multiple_of(r * BS, BS), BS)
            acc[at, :] += prod

    for c in late:
        c.wait()

    @pl.loop(0, NODES // CHUNK)
    def _(i):
        base = pl.multiple_of(i * CHUNK, CHUNK)
        at = pl.ds(base, CHUNK)
        agg = acc[at, :].astype(BF)
        pre = jnp.dot(agg, weight[...], preferred_element_type=F32) + bias[...]
        sig = jax.nn.sigmoid(pre)
        keep = lax.broadcasted_iota(jnp.int32, (CHUNK, F), 0) + base < alive
        outbuf[at, :] = jnp.where(keep, pre * sig, F32(0.0)).astype(BF)
        pltpu.make_async_copy(outbuf.at[at], output.at[at], osems.at[0]).start()
        g = grads[at, :].astype(F32)
        dpre = jnp.where(keep, g * sig * (1.0 + pre * (1.0 - sig)), F32(0.0)).astype(BF)
        bacc[...] += jnp.sum(dpre.astype(F32).reshape(CHUNK // 8, 8, F), 0)
        wacc[...] += lax.dot_general(agg, dpre, (((0,), (0,)), ((), ())), preferred_element_type=F32)
        back[at, :] = lax.dot_general(
            dpre, weight[...], (((1,), (1,)), ((), ())), preferred_element_type=F32
        ).astype(BF)

    for p in range(PEERS):
        a, c = p // 4, p % 4
        terms[p, 0:16, :] = wacc[a * 16 : (a + 1) * 16, c * BS : (c + 1) * BS].astype(BF)
    total = jnp.sum(bacc[...], 0, keepdims=True)
    high = total.astype(BF).astype(F32)
    low = total - high
    lines = jnp.concatenate(
        [high[:, c * BS : (c + 1) * BS] for c in range(4)] + [low[:, c * BS : (c + 1) * BS] for c in range(4)], 0
    ).astype(BF)
    terms[:, 16:24, :] = jnp.broadcast_to(lines[None], (PEERS, 8, BS))

    @pl.loop(0, BLK // UNROLL)
    def _(i):
        prods, targets = [], []
        for u in range(UNROLL):
            b = i * UNROLL + u
            prods.append(
                lax.dot_general(
                    adj[b], block(back, rows[0, b]), (((0,), (0,)), ((), ())), preferred_element_type=F32
                )
            )
            targets.append(jnp.where(b < live, cols[0, b], ECB))
        for prod, c in zip(prods, targets):
            at = pl.ds(pl.multiple_of(c * BS, BS), BS)
            spread[at, :] += prod

    for k, ret in enumerate((ret0, ret1, ret2, ret3)):
        ret[...] = spread[NODES + k * HALO : NODES + (k + 1) * HALO, :].astype(BF)
    low_rows = pltpu.make_async_copy(spread.at[pl.ds(0, HALF)], own, osems.at[1])
    low_rows.start()
    pltpu.make_async_copy(outbuf, output, osems.at[0]).wait()

    @pl.loop(HALF // BS, RB)
    def _(r):
        at = pl.ds(pl.multiple_of(r * BS, BS), BS)
        line = lax.broadcasted_iota(jnp.int32, (BS, F), 0) + r * BS
        outbuf[at, :] = jnp.where(line < alive, spread[at, :], F32(0.0)).astype(BF)

    high_rows = pltpu.make_async_copy(
        outbuf.at[pl.ds(HALF, HALF)], input_grad.at[pl.ds(HALF, HALF)], osems.at[2]
    )
    high_rows.start()
    high_rows.wait()
    low_rows.wait()


def main(rows, cols, count, nodes, features, adjacency, halos, weight, bias, out_grad):
    smem = pl.BlockSpec(memory_space=pltpu.SMEM)
    vmem = pl.BlockSpec(memory_space=pltpu.VMEM)
    hbm = pl.BlockSpec(memory_space=pl.ANY)
    return pl.pallas_call(
        main_kernel,
        in_specs=[smem] * 4 + [hbm] * 7 + [vmem, hbm],
        out_specs=[hbm] * 3 + [vmem] * 5,
        out_shape=[
            jax.ShapeDtypeStruct((NODES, F), BF),
            jax.ShapeDtypeStruct((NODES, F), BF),
            jax.ShapeDtypeStruct((HALF, F), F32),
        ]
        + [jax.ShapeDtypeStruct((HALO, F), BF)] * 4
        + [jax.ShapeDtypeStruct((PEERS, 24, BS), BF)],
        scratch_shapes=[
            pltpu.VMEM((ECB * BS, F), BF),
            pltpu.VMEM((BLK, BS, BS), BF),
            pltpu.VMEM(((RB + 1) * BS, F), F32),
            pltpu.VMEM(((ECB + 1) * BS, F), F32),
            pltpu.VMEM((F, F), BF),
            pltpu.VMEM((NODES, F), BF),
            pltpu.VMEM((NODES, F), BF),
            pltpu.VMEM((NODES, F), BF),
            pltpu.VMEM((F, F), F32),
            pltpu.VMEM((8, F), F32),
            pltpu.SemaphoreType.DMA((8,)),
            pltpu.SemaphoreType.DMA((3,)),
        ],
        compiler_params=pltpu.CompilerParams(vmem_limit_bytes=VMEM_BYTES),
        name="main",
    )(rows, cols, count, nodes, features, adjacency, *halos, weight, bias, out_grad)


def finish_kernel(picks, own, r0, r1, r2, r3, held, input_grad, buf, sem):
    line = lax.broadcasted_iota(jnp.int32, (HALO, HALO), 0)
    copies = []
    for i in range(HALF // HALO):
        hit = [
            jnp.where(line + i * HALO == picks[k : k + 1, :], F32(1.0), F32(0.0)).astype(BF) for k in range(4)
        ]
        got = own[i * HALO : (i + 1) * HALO, :]
        for k, r in enumerate((r0, r1, r2, r3)):
            got = got + jnp.dot(hit[k], r[...], preferred_element_type=F32)
        buf[i * HALO : (i + 1) * HALO, :] = got.astype(BF)
        at = pl.ds(i * HALO, HALO)
        copies.append(pltpu.make_async_copy(buf.at[at], input_grad.at[at], sem.at[i]))
        copies[-1].start()
    for c in copies:
        c.wait()


def finish(picks, own, returned, input_grad):
    vmem = pl.BlockSpec(memory_space=pltpu.VMEM)
    hbm = pl.BlockSpec(memory_space=pl.ANY)
    return pl.pallas_call(
        finish_kernel,
        in_specs=[vmem] * 6 + [hbm],
        out_specs=hbm,
        out_shape=jax.ShapeDtypeStruct((NODES, F), BF),
        input_output_aliases={6: 0},
        scratch_shapes=[pltpu.VMEM((HALF, F), BF), pltpu.SemaphoreType.DMA((HALF // HALO,))],
        compiler_params=pltpu.CompilerParams(vmem_limit_bytes=VMEM_BYTES),
        name="finish",
    )(picks, own, *returned, input_grad)


def exchange(parts):
    got = []
    for k in range(4):
        axis = AXES[k // 2]
        count = lax.axis_size(axis)
        if k % 2 == 0:
            pairs = [(i, i + 1) for i in range(count - 1)]
        else:
            pairs = [(i + 1, i) for i in range(count - 1)]
        got.append(lax.ppermute(parts[k ^ 1], axis, pairs))
    return got


def local(features, adjacency, block_rows, block_cols, block_count, node_count, halo_index, weight, bias, out_grad):
    picks = halo_index.reshape(4, HALO)
    halos = exchange(pack(picks, features))
    output, partial_grad, own, r0, r1, r2, r3, terms = main(
        block_rows, block_cols, block_count, node_count, features, adjacency, halos, weight, bias.reshape(1, F), out_grad
    )
    returned = exchange((r0, r1, r2, r3))
    scale = 1.0 / math.sqrt(NODES * PEERS)
    gathered = lax.all_to_all(terms, AXES, 0, 0, tiled=True).astype(F32)
    sums = jnp.sum(gathered, 0) * scale
    share = sums[0:16].astype(BF)
    bias_grad = (sums[16:20] + sums[20:24]).reshape(F)
    spread_out = lax.all_to_all(jnp.broadcast_to(share[None], (PEERS, 16, BS)), AXES, 0, 0, tiled=True)
    weight_grad = spread_out.astype(F32).reshape(32, 4, 16, BS).transpose(0, 2, 1, 3).reshape(F, F)
    input_grad = finish(picks, own, returned, partial_grad)
    return (output, input_grad, weight_grad, bias_grad)


def solution(mesh):
    placed = (
        P(AXES, None),
        P(AXES, None, None),
        P(AXES, None),
        P(AXES, None),
        P(AXES),
        P(AXES),
        P(AXES, None, None),
        P(),
        P(),
        P(AXES, None),
    )
    return jax.shard_map(
        local,
        mesh=mesh,
        in_specs=placed,
        out_specs=(P(AXES, None), P(AXES, None), P(), P()),
        check_vma=False,
    )
```

```python
import math

import jax
import jax.numpy as jnp
from jax import lax
from jax.experimental import pallas as pl
from jax.experimental.pallas import tpu as pltpu
from jax.sharding import PartitionSpec as P

F = 512
BS = 128
NODES = 4096
HALO = 256
RB = 32
ECB = 40
BLK = 96
HALF = 2048
CHUNK = 1024
PEERS = 128
UNROLL = 16
BF = jnp.bfloat16
F32 = jnp.float32
VMEM_BYTES = 24 * 1024 * 1024
VMEM_OWN = 20 * 1024 * 1024
VMEM_DENSE = 36 * 1024 * 1024
VMEM_BACK = 28 * 1024 * 1024
AXES = ("wide", "narrow")


SMEM = pl.BlockSpec(memory_space=pltpu.SMEM)
VMEM = pl.BlockSpec(memory_space=pltpu.VMEM)
HBM = pl.BlockSpec(memory_space=pl.ANY)


def cost(us):
    return pl.CostEstimate(flops=int(us * 1e9), bytes_accessed=int(us * 3e6), transcendentals=0)


def held(x):
    return pltpu.with_memory_space_constraint(x, pltpu.VMEM)


def in_hbm(x):
    return pltpu.with_memory_space_constraint(x, pltpu.HBM)


def pack_kernel(picks, feats_in, out0, out1, out2, out3, onehot, feats, sem):
    outs = (out0, out1, out2, out3)
    load = pltpu.make_async_copy(feats_in.at[pl.ds(0, HALF)], feats, sem.at[0])
    load.start()
    lane = lax.broadcasted_iota(jnp.int32, (BS, BS), 1)

    def build(k):
        for h in range(2):
            row = picks[k : k + 1, h * BS : (h + 1) * BS]
            t = jnp.transpose(jnp.broadcast_to(row.astype(F32), (BS, BS))).astype(jnp.int32)
            for c in range(HALF // BS):
                hit = jnp.where(t == lane + c * BS, F32(1.0), F32(0.0)).astype(BF)
                onehot[k * HALO + h * BS : k * HALO + (h + 1) * BS, c * BS : (c + 1) * BS] = hit

    build(0)
    build(1)
    load.wait()
    for k in range(4):
        if k >= 2:
            build(k)
        outs[k][...] = jnp.dot(onehot[k * HALO : (k + 1) * HALO, :], feats[...], preferred_element_type=F32).astype(BF)


def pack(picks, features):
    return pl.pallas_call(
        pack_kernel,
        in_specs=[VMEM, HBM],
        out_specs=[VMEM] * 4,
        out_shape=[jax.ShapeDtypeStruct((HALO, F), BF)] * 4,
        scratch_shapes=[
            pltpu.VMEM((4 * HALO, HALF), BF),
            pltpu.VMEM((HALF, F), BF),
            pltpu.SemaphoreType.DMA((1,)),
        ],
        compiler_params=pltpu.CompilerParams(vmem_limit_bytes=VMEM_BYTES),
        cost_estimate=cost(3),
        name="pack",
    )(picks, in_hbm(features))


def block(ref, i):
    return ref[pl.ds(pl.multiple_of(i * BS, BS), BS), :]


def tail_mask(ref, start, alive):
    @pl.loop(start, RB)
    def _(r):
        at = pl.ds(pl.multiple_of(r * BS, BS), BS)
        line = lax.broadcasted_iota(jnp.int32, (BS, F), 0) + r * BS
        ref[at, :] = jnp.where(line < alive, ref[at, :].astype(F32), F32(0.0)).astype(BF)


def zero_blocks(ref, count):
    @pl.loop(0, count)
    def _(r):
        ref[pl.ds(pl.multiple_of(r * BS, BS), BS), :] = jnp.zeros((BS, F), F32)


def slot_list(table, rows, cols, live, halo, spare):
    def step(b, n):
        c = cols[0, b]
        take = jnp.logical_and(b < live, (c >= RB) == (halo == 1))
        table[n] = b + (rows[0, b] << 8) + (c << 16)
        return n + take.astype(jnp.int32)

    n = lax.fori_loop(0, BLK, step, jnp.int32(0))
    for u in range(UNROLL):
        table[n + u] = jnp.int32(spare)
    return (n + UNROLL - 1) // UNROLL


def unpack(code):
    return code & 255, (code >> 8) & 255, code >> 16


def own_kernel(rows, cols, count, nodes, feats, adj_in, acc, adj, ext, table, sems):
    loads = [
        pltpu.make_async_copy(adj_in, adj, sems.at[0]),
        pltpu.make_async_copy(feats, ext, sems.at[1]),
    ]
    for c in loads:
        c.start()
    zero_blocks(acc, RB + 1)
    groups = slot_list(table, rows, cols, count[0], 0, RB << 8)
    for c in loads:
        c.wait()
    tail_mask(ext, nodes[0] // BS, nodes[0])

    @pl.loop(0, groups)
    def _(i):
        prods, targets = [], []
        for u in range(UNROLL):
            b, r, c = unpack(table[i * UNROLL + u])
            prods.append(jnp.dot(adj[b], block(ext, c), preferred_element_type=F32))
            targets.append(r)
        for prod, r in zip(prods, targets):
            at = pl.ds(pl.multiple_of(r * BS, BS), BS)
            acc[at, :] += prod


def own_part(rows, cols, count, nodes, features, adjacency):
    return pl.pallas_call(
        own_kernel,
        in_specs=[SMEM] * 4 + [HBM] * 2,
        out_specs=[VMEM] * 2,
        out_shape=[pltpu.VMEM(((RB + 1) * BS, F), F32), pltpu.VMEM((BLK, BS, BS), BF)],
        scratch_shapes=[
            pltpu.VMEM((NODES, F), BF),
            pltpu.SMEM((BLK + UNROLL,), jnp.int32),
            pltpu.SemaphoreType.DMA((2,)),
        ],
        compiler_params=pltpu.CompilerParams(vmem_limit_bytes=VMEM_OWN),
        cost_estimate=cost(8),
        name="own_part",
    )(rows, cols, count, nodes, in_hbm(features), in_hbm(adjacency))


def dense_kernel(
    rows, cols, count, nodes, acc_in, adj, h0, h1, h2, h3, weight, bias, grads_in,
    acc, output, back_out, ret0, ret1, ret2, ret3, terms,
    back, received, spread, grads, outbuf, wacc, bacc, table, gsems, osems,
):
    alive = nodes[0]
    halos = (h0, h1, h2, h3)

    def grad_copy(i):
        at = pl.ds(pl.multiple_of(i * CHUNK, CHUNK), CHUNK)
        return pltpu.make_async_copy(grads_in.at[at], grads.at[at], gsems.at[i])

    for i in range(NODES // CHUNK):
        grad_copy(i).start()
    groups = slot_list(table, rows, cols, count[0], 1, (RB << 8) + (ECB << 16))
    zero_blocks(spread, ECB - RB + 1)
    wacc[...] = jnp.zeros_like(wacc)
    bacc[...] = jnp.zeros_like(bacc)
    for k in range(4):
        hal_at = pl.ds(k * HALO, HALO)
        received[hal_at, :] = halos[k][...]

    @pl.loop(0, groups)
    def _(i):
        prods, targets = [], []
        for u in range(UNROLL):
            b, r, c = unpack(table[i * UNROLL + u])
            prods.append(jnp.dot(adj[b], block(received, c - RB), preferred_element_type=F32))
            targets.append(r)
        for prod, r in zip(prods, targets):
            at = pl.ds(pl.multiple_of(r * BS, BS), BS)
            acc[at, :] += prod

    @pl.loop(0, NODES // CHUNK)
    def _(i):
        base = pl.multiple_of(i * CHUNK, CHUNK)
        at = pl.ds(base, CHUNK)
        grad_copy(i).wait()
        agg = acc[at, :].astype(BF)
        pre = jnp.dot(agg, weight[...], preferred_element_type=F32) + bias[...]
        sig = jax.nn.sigmoid(pre)
        keep = lax.broadcasted_iota(jnp.int32, (CHUNK, F), 0) + base < alive
        outbuf[at, :] = jnp.where(keep, pre * sig, F32(0.0)).astype(BF)
        pltpu.make_async_copy(outbuf.at[at], output.at[at], osems.at[0]).start()
        g = grads[at, :].astype(F32)
        dpre = jnp.where(keep, g * sig * (1.0 + pre * (1.0 - sig)), F32(0.0)).astype(BF)
        bacc[...] += jnp.sum(dpre.astype(F32).reshape(CHUNK // 8, 8, F), 0)
        wacc[...] += lax.dot_general(agg, dpre, (((0,), (0,)), ((), ())), preferred_element_type=F32)
        back[at, :] = lax.dot_general(
            dpre, weight[...], (((1,), (1,)), ((), ())), preferred_element_type=F32
        ).astype(BF)
        pltpu.make_async_copy(back.at[at], back_out.at[at], osems.at[1]).start()

    for p in range(PEERS):
        for t in range(2):
            a, c = p // 2, p % 2 * 2 + t
            terms[p, 8 * t : 8 * t + 8, :] = wacc[a * 8 : (a + 1) * 8, c * BS : (c + 1) * BS].astype(BF)
    total = jnp.sum(bacc[...], 0, keepdims=True)
    high = total.astype(BF).astype(F32)
    low = total - high
    lines = jnp.concatenate(
        [high[:, c * BS : (c + 1) * BS] for c in range(4)] + [low[:, c * BS : (c + 1) * BS] for c in range(4)], 0
    ).astype(BF)
    terms[:, 16:24, :] = jnp.broadcast_to(lines[None], (PEERS, 8, BS))

    @pl.loop(0, groups)
    def _(i):
        prods, targets = [], []
        for u in range(UNROLL):
            b, r, c = unpack(table[i * UNROLL + u])
            r = jnp.where(r < RB, r, 0)
            prods.append(
                lax.dot_general(adj[b], block(back, r), (((0,), (0,)), ((), ())), preferred_element_type=F32)
            )
            targets.append(c - RB)
        for prod, c in zip(prods, targets):
            at = pl.ds(pl.multiple_of(c * BS, BS), BS)
            spread[at, :] += prod

    for k, ret in enumerate((ret0, ret1, ret2, ret3)):
        ret[...] = spread[k * HALO : (k + 1) * HALO, :].astype(BF)
    pltpu.make_async_copy(outbuf, output, osems.at[0]).wait()
    pltpu.make_async_copy(back, back_out, osems.at[1]).wait()


def dense_part(rows, cols, count, nodes, acc, adj, halos, weight, bias, out_grad):
    return pl.pallas_call(
        dense_kernel,
        in_specs=[SMEM] * 4 + [VMEM] * 8 + [HBM],
        out_specs=[VMEM, HBM, HBM] + [VMEM] * 5,
        out_shape=[
            pltpu.VMEM(((RB + 1) * BS, F), F32),
            jax.ShapeDtypeStruct((NODES, F), BF),
            jax.ShapeDtypeStruct((NODES, F), BF),
        ]
        + [jax.ShapeDtypeStruct((HALO, F), BF)] * 4
        + [jax.ShapeDtypeStruct((PEERS, 24, BS), BF)],
        input_output_aliases={4: 0},
        scratch_shapes=[
            pltpu.VMEM((NODES, F), BF),
            pltpu.VMEM(((ECB - RB + 1) * BS, F), BF),
            pltpu.VMEM(((ECB - RB + 1) * BS, F), F32),
            pltpu.VMEM((NODES, F), BF),
            pltpu.VMEM((NODES, F), BF),
            pltpu.VMEM((F, F), F32),
            pltpu.VMEM((8, F), F32),
            pltpu.SMEM((BLK + UNROLL,), jnp.int32),
            pltpu.SemaphoreType.DMA((NODES // CHUNK,)),
            pltpu.SemaphoreType.DMA((2,)),
        ],
        compiler_params=pltpu.CompilerParams(vmem_limit_bytes=VMEM_DENSE),
        cost_estimate=cost(16),
        name="dense_part",
    )(rows, cols, count, nodes, held(acc), held(adj), *halos, weight, bias, in_hbm(out_grad))[1:]


def back_kernel(
    rows, cols, count, nodes, adj_in, back_in, picks, r0, r1, r2, r3, input_grad, adj, back, spread, outbuf, table, sems
):
    alive = nodes[0]
    loads = [
        pltpu.make_async_copy(adj_in, adj, sems.at[2]),
        pltpu.make_async_copy(back_in, back, sems.at[3]),
    ]
    for c in loads:
        c.start()
    zero_blocks(spread, RB + 1)
    groups = slot_list(table, rows, cols, count[0], 0, RB << 16)
    for c in loads:
        c.wait()

    @pl.loop(0, groups)
    def _(i):
        prods, targets = [], []
        for u in range(UNROLL):
            b, r, c = unpack(table[i * UNROLL + u])
            prods.append(
                lax.dot_general(adj[b], block(back, r), (((0,), (0,)), ((), ())), preferred_element_type=F32)
            )
            targets.append(c)
        for prod, c in zip(prods, targets):
            at = pl.ds(pl.multiple_of(c * BS, BS), BS)
            spread[at, :] += prod

    @pl.loop(HALF // BS, RB)
    def _(r):
        at = pl.ds(pl.multiple_of(r * BS, BS), BS)
        line = lax.broadcasted_iota(jnp.int32, (BS, F), 0) + r * BS
        outbuf[at, :] = jnp.where(line < alive, spread[at, :], F32(0.0)).astype(BF)

    top = pltpu.make_async_copy(outbuf.at[pl.ds(HALF, HALF)], input_grad.at[pl.ds(HALF, HALF)], sems.at[0])
    top.start()
    line = lax.broadcasted_iota(jnp.int32, (HALO, HALO), 0)

    @pl.loop(0, HALF // HALO)
    def _(i):
        at = pl.ds(pl.multiple_of(i * HALO, HALO), HALO)
        got = spread[at, :]
        for k, r in enumerate((r0, r1, r2, r3)):
            hit = jnp.where(line + i * HALO == picks[k : k + 1, :], F32(1.0), F32(0.0)).astype(BF)
            got = got + jnp.dot(hit, r[...], preferred_element_type=F32)
        outbuf[at, :] = got.astype(BF)
        pltpu.make_async_copy(outbuf.at[at], input_grad.at[at], sems.at[1]).start()

    low = pl.ds(0, HALF)
    pltpu.make_async_copy(outbuf.at[low], input_grad.at[low], sems.at[1]).wait()
    top.wait()


def back_part(rows, cols, count, nodes, adj, back, picks, returned):
    return pl.pallas_call(
        back_kernel,
        in_specs=[SMEM] * 4 + [HBM] * 2 + [VMEM] * 5,
        out_specs=HBM,
        out_shape=jax.ShapeDtypeStruct((NODES, F), BF),
        scratch_shapes=[
            pltpu.VMEM((BLK, BS, BS), BF),
            pltpu.VMEM((NODES, F), BF),
            pltpu.VMEM(((RB + 1) * BS, F), F32),
            pltpu.VMEM((NODES, F), BF),
            pltpu.SMEM((BLK + UNROLL,), jnp.int32),
            pltpu.SemaphoreType.DMA((4,)),
        ],
        compiler_params=pltpu.CompilerParams(vmem_limit_bytes=VMEM_BACK),
        cost_estimate=cost(12),
        name="back_part",
    )(rows, cols, count, nodes, in_hbm(adj), in_hbm(back), picks, *returned)


def exchange(parts):
    got = []
    for k in range(4):
        axis = AXES[k // 2]
        count = lax.axis_size(axis)
        if k % 2 == 0:
            pairs = [(i, i + 1) for i in range(count - 1)]
        else:
            pairs = [(i + 1, i) for i in range(count - 1)]
        got.append(lax.ppermute(parts[k ^ 1], axis, pairs))
    return got


def local(features, adjacency, block_rows, block_cols, block_count, node_count, halo_index, weight, bias, out_grad):
    picks = halo_index.reshape(4, HALO)
    tables = (block_rows, block_cols, block_count, node_count)
    packed = pack(picks, features)
    packed, adjacency = lax.optimization_barrier((packed, adjacency))
    acc, adj = own_part(*tables, features, adjacency)
    halos = exchange(packed)
    output, back, r0, r1, r2, r3, terms = dense_part(
        *tables, acc, adj, halos, weight, bias.reshape(1, F), out_grad
    )
    returned = exchange((r0, r1, r2, r3))
    scale = 1.0 / math.sqrt(NODES * PEERS)
    gathered = lax.all_to_all(terms, AXES, 0, 0, tiled=True).astype(F32)
    sums = jnp.sum(gathered, 0) * scale
    share = sums[0:16].astype(BF)
    bias_grad = (sums[16:20] + sums[20:24]).reshape(F)
    tiles = jnp.broadcast_to(share[None], (PEERS, 16, BS))
    tiles, picks = lax.optimization_barrier((tiles, picks))
    tiles = lax.all_to_all(tiles, AXES, 0, 0, tiled=True)
    weight_grad = tiles.astype(F32).reshape(64, 4, 8, BS).transpose(0, 2, 1, 3).reshape(F, F)
    input_grad = back_part(*tables, adjacency, back, picks, returned)
    return (output, input_grad, weight_grad, bias_grad)


def solution(mesh):
    placed = (
        P(AXES, None),
        P(AXES, None, None),
        P(AXES, None),
        P(AXES, None),
        P(AXES),
        P(AXES),
        P(AXES, None, None),
        P(),
        P(),
        P(AXES, None),
    )
    return jax.shard_map(
        local,
        mesh=mesh,
        in_specs=placed,
        out_specs=(P(AXES, None), P(AXES, None), P(), P()),
        check_vma=False,
    )
```

```python
import math

import jax
import jax.numpy as jnp
from jax import lax
from jax.experimental import pallas as pl
from jax.experimental.pallas import tpu as pltpu
from jax.sharding import PartitionSpec as P

F = 512
BS = 128
NODES = 4096
HALO = 256
RB = 32
ECB = 40
BLK = 96
HALF = 2048
CHUNK = 1024
PEERS = 128
UNROLL = 16
FEW = 8
BF = jnp.bfloat16
F32 = jnp.float32
VMEM_BYTES = 24 * 1024 * 1024
VMEM_OWN = 20 * 1024 * 1024
VMEM_DENSE = 36 * 1024 * 1024
VMEM_BACK = 28 * 1024 * 1024
AXES = ("wide", "narrow")


SMEM = pl.BlockSpec(memory_space=pltpu.SMEM)
VMEM = pl.BlockSpec(memory_space=pltpu.VMEM)
HBM = pl.BlockSpec(memory_space=pl.ANY)


def cost(us):
    return pl.CostEstimate(flops=int(us * 1e9), bytes_accessed=int(us * 3e6), transcendentals=0)


def held(x):
    return pltpu.with_memory_space_constraint(x, pltpu.VMEM)


def in_hbm(x):
    return pltpu.with_memory_space_constraint(x, pltpu.HBM)


def flips():
    return 1 - (lax.axis_index("wide") & 1), 1 - (lax.axis_index("narrow") & 1)


def pick_row(picks, k, flip):
    return picks[pl.ds((k & 2) + ((k & 1) ^ flip[k // 2]), 1), :]


def pack_kernel(picks, feats_in, out0, out1, out2, out3, onehot, feats, sem):
    outs = (out0, out1, out2, out3)
    load = pltpu.make_async_copy(feats_in.at[pl.ds(0, HALF)], feats, sem.at[0])
    load.start()
    lane = lax.broadcasted_iota(jnp.int32, (BS, BS), 1)

    flip = flips()

    def build(k):
        line = pick_row(picks, k, flip)
        for h in range(2):
            row = line[:, h * BS : (h + 1) * BS]
            t = jnp.transpose(jnp.broadcast_to(row.astype(F32), (BS, BS))).astype(jnp.int32)
            for c in range(HALF // BS):
                hit = jnp.where(t == lane + c * BS, F32(1.0), F32(0.0)).astype(BF)
                onehot[k * HALO + h * BS : k * HALO + (h + 1) * BS, c * BS : (c + 1) * BS] = hit

    build(0)
    build(1)
    load.wait()
    for k in range(4):
        if k >= 2:
            build(k)
        outs[k][...] = jnp.dot(onehot[k * HALO : (k + 1) * HALO, :], feats[...], preferred_element_type=F32).astype(BF)


def pack(picks, features):
    return pl.pallas_call(
        pack_kernel,
        in_specs=[VMEM, HBM],
        out_specs=[VMEM] * 4,
        out_shape=[jax.ShapeDtypeStruct((HALO, F), BF)] * 4,
        scratch_shapes=[
            pltpu.VMEM((4 * HALO, HALF), BF),
            pltpu.VMEM((HALF, F), BF),
            pltpu.SemaphoreType.DMA((1,)),
        ],
        compiler_params=pltpu.CompilerParams(vmem_limit_bytes=VMEM_BYTES),
        cost_estimate=cost(3),
        name="pack",
    )(picks, in_hbm(features))


def block(ref, i):
    return ref[pl.ds(pl.multiple_of(i * BS, BS), BS), :]


def tail_mask(ref, start, alive):
    @pl.loop(start, RB)
    def _(r):
        at = pl.ds(pl.multiple_of(r * BS, BS), BS)
        line = lax.broadcasted_iota(jnp.int32, (BS, F), 0) + r * BS
        ref[at, :] = jnp.where(line < alive, ref[at, :].astype(F32), F32(0.0)).astype(BF)


def zero_blocks(ref, count):
    @pl.loop(0, count)
    def _(r):
        ref[pl.ds(pl.multiple_of(r * BS, BS), BS), :] = jnp.zeros((BS, F), F32)


def slot_list(table, rows, cols, live, halo, spare, unroll):
    flip = flips()

    def step(b, n):
        c = cols[0, b]
        take = jnp.logical_and(b < live, (c >= RB) == (halo == 1))
        turn = jnp.where(c < RB, 0, jnp.where(c < RB + 4, flip[0], flip[1]) * 2)
        table[n] = b + (rows[0, b] << 8) + ((c ^ turn) << 16)
        return n + take.astype(jnp.int32)

    n = lax.fori_loop(0, BLK, step, jnp.int32(0))
    for u in range(unroll):
        table[n + u] = jnp.int32(spare)
    return (n + unroll - 1) // unroll


def unpack(code):
    return code & 255, (code >> 8) & 255, code >> 16


def own_kernel(rows, cols, count, nodes, feats, adj_in, acc, adj, ext, table, sems):
    loads = [
        pltpu.make_async_copy(adj_in, adj, sems.at[0]),
        pltpu.make_async_copy(feats, ext, sems.at[1]),
    ]
    for c in loads:
        c.start()
    zero_blocks(acc, RB + 1)
    groups = slot_list(table, rows, cols, count[0], 0, RB << 8, UNROLL)
    for c in loads:
        c.wait()
    tail_mask(ext, nodes[0] // BS, nodes[0])

    @pl.loop(0, groups)
    def _(i):
        prods, targets = [], []
        for u in range(UNROLL):
            b, r, c = unpack(table[i * UNROLL + u])
            prods.append(jnp.dot(adj[b], block(ext, c), preferred_element_type=F32))
            targets.append(r)
        for prod, r in zip(prods, targets):
            at = pl.ds(pl.multiple_of(r * BS, BS), BS)
            acc[at, :] += prod


def own_part(rows, cols, count, nodes, features, adjacency):
    return pl.pallas_call(
        own_kernel,
        in_specs=[SMEM] * 4 + [HBM] * 2,
        out_specs=[VMEM] * 2,
        out_shape=[pltpu.VMEM(((RB + 1) * BS, F), F32), pltpu.VMEM((BLK, BS, BS), BF)],
        scratch_shapes=[
            pltpu.VMEM((NODES, F), BF),
            pltpu.SMEM((BLK + UNROLL,), jnp.int32),
            pltpu.SemaphoreType.DMA((2,)),
        ],
        compiler_params=pltpu.CompilerParams(vmem_limit_bytes=VMEM_OWN),
        cost_estimate=cost(8),
        name="own_part",
    )(rows, cols, count, nodes, in_hbm(features), in_hbm(adjacency))


def dense_kernel(
    rows, cols, count, nodes, acc_in, adj, h0, h1, h2, h3, weight, bias, grads_in,
    acc, output, back_out, ret0, ret1, ret2, ret3, terms, lines_out,
    back, received, spread, grads, outbuf, wacc, bacc, table, gsems, osems,
):
    alive = nodes[0]
    halos = (h0, h1, h2, h3)

    def grad_copy(i):
        at = pl.ds(pl.multiple_of(i * CHUNK, CHUNK), CHUNK)
        return pltpu.make_async_copy(grads_in.at[at], grads.at[at], gsems.at[i])

    for i in range(NODES // CHUNK):
        grad_copy(i).start()
    groups = slot_list(table, rows, cols, count[0], 1, (RB << 8) + (ECB << 16), FEW)
    zero_blocks(spread, ECB - RB + 1)
    wacc[...] = jnp.zeros_like(wacc)
    bacc[...] = jnp.zeros_like(bacc)
    for k in range(4):
        hal_at = pl.ds(k * HALO, HALO)
        received[hal_at, :] = halos[k][...]

    @pl.loop(0, groups)
    def _(i):
        prods, targets = [], []
        for u in range(FEW):
            b, r, c = unpack(table[i * FEW + u])
            prods.append(jnp.dot(adj[b], block(received, c - RB), preferred_element_type=F32))
            targets.append(r)
        for prod, r in zip(prods, targets):
            at = pl.ds(pl.multiple_of(r * BS, BS), BS)
            acc[at, :] += prod

    @pl.loop(0, NODES // CHUNK)
    def _(i):
        base = pl.multiple_of(i * CHUNK, CHUNK)
        at = pl.ds(base, CHUNK)
        grad_copy(i).wait()
        agg = acc[at, :].astype(BF)
        pre = jnp.dot(agg, weight[...], preferred_element_type=F32) + bias[...]
        sig = jax.nn.sigmoid(pre)
        keep = lax.broadcasted_iota(jnp.int32, (CHUNK, F), 0) + base < alive
        outbuf[at, :] = jnp.where(keep, pre * sig, F32(0.0)).astype(BF)
        pltpu.make_async_copy(outbuf.at[at], output.at[at], osems.at[0]).start()
        g = grads[at, :].astype(F32)
        dpre = jnp.where(keep, g * sig * (1.0 + pre * (1.0 - sig)), F32(0.0)).astype(BF)
        bacc[...] += jnp.sum(dpre.astype(F32).reshape(CHUNK // 8, 8, F), 0)
        wacc[...] += lax.dot_general(agg, dpre, (((0,), (0,)), ((), ())), preferred_element_type=F32)
        back[at, :] = lax.dot_general(
            dpre, weight[...], (((1,), (1,)), ((), ())), preferred_element_type=F32
        ).astype(BF)
        pltpu.make_async_copy(back.at[at], back_out.at[at], osems.at[1]).start()

    for p in range(PEERS):
        for t in range(2):
            a, c = p // 2, p % 2 * 2 + t
            terms[p, 8 * t : 8 * t + 8, :] = wacc[a * 8 : (a + 1) * 8, c * BS : (c + 1) * BS].astype(BF)
    total = jnp.sum(bacc[...], 0, keepdims=True)
    high = total.astype(BF).astype(F32)
    low = total - high
    lines = jnp.concatenate(
        [high[:, c * BS : (c + 1) * BS] for c in range(4)] + [low[:, c * BS : (c + 1) * BS] for c in range(4)], 0
    ).astype(BF)
    lines_out[...] = lines

    @pl.loop(0, groups)
    def _(i):
        prods, targets = [], []
        for u in range(FEW):
            b, r, c = unpack(table[i * FEW + u])
            r = jnp.where(r < RB, r, 0)
            prods.append(
                lax.dot_general(adj[b], block(back, r), (((0,), (0,)), ((), ())), preferred_element_type=F32)
            )
            targets.append(c - RB)
        for prod, c in zip(prods, targets):
            at = pl.ds(pl.multiple_of(c * BS, BS), BS)
            spread[at, :] += prod

    for k, ret in enumerate((ret0, ret1, ret2, ret3)):
        ret[...] = spread[k * HALO : (k + 1) * HALO, :].astype(BF)
    pltpu.make_async_copy(outbuf, output, osems.at[0]).wait()
    pltpu.make_async_copy(back, back_out, osems.at[1]).wait()


def dense_part(rows, cols, count, nodes, acc, adj, halos, weight, bias, out_grad):
    return pl.pallas_call(
        dense_kernel,
        in_specs=[SMEM] * 4 + [VMEM] * 8 + [HBM],
        out_specs=[VMEM, HBM, HBM] + [VMEM] * 6,
        out_shape=[
            pltpu.VMEM(((RB + 1) * BS, F), F32),
            jax.ShapeDtypeStruct((NODES, F), BF),
            jax.ShapeDtypeStruct((NODES, F), BF),
        ]
        + [jax.ShapeDtypeStruct((HALO, F), BF)] * 4
        + [jax.ShapeDtypeStruct((PEERS, 16, BS), BF), jax.ShapeDtypeStruct((8, BS), BF)],
        input_output_aliases={4: 0},
        scratch_shapes=[
            pltpu.VMEM((NODES, F), BF),
            pltpu.VMEM(((ECB - RB + 1) * BS, F), BF),
            pltpu.VMEM(((ECB - RB + 1) * BS, F), F32),
            pltpu.VMEM((NODES, F), BF),
            pltpu.VMEM((NODES, F), BF),
            pltpu.VMEM((F, F), F32),
            pltpu.VMEM((8, F), F32),
            pltpu.SMEM((BLK + UNROLL,), jnp.int32),
            pltpu.SemaphoreType.DMA((NODES // CHUNK,)),
            pltpu.SemaphoreType.DMA((2,)),
        ],
        compiler_params=pltpu.CompilerParams(vmem_limit_bytes=VMEM_DENSE),
        cost_estimate=cost(16),
        name="dense_part",
    )(rows, cols, count, nodes, held(acc), held(adj), *halos, weight, bias, in_hbm(out_grad))[1:]


def back_kernel(
    rows, cols, count, nodes, adj_in, back_in, picks, r0, r1, r2, r3, input_grad, adj, back, spread, outbuf, table, sems
):
    alive = nodes[0]
    loads = [
        pltpu.make_async_copy(adj_in, adj, sems.at[2]),
        pltpu.make_async_copy(back_in, back, sems.at[3]),
    ]
    for c in loads:
        c.start()
    zero_blocks(spread, RB + 1)
    groups = slot_list(table, rows, cols, count[0], 0, RB << 16, UNROLL)
    for c in loads:
        c.wait()

    @pl.loop(0, groups)
    def _(i):
        prods, targets = [], []
        for u in range(UNROLL):
            b, r, c = unpack(table[i * UNROLL + u])
            prods.append(
                lax.dot_general(adj[b], block(back, r), (((0,), (0,)), ((), ())), preferred_element_type=F32)
            )
            targets.append(c)
        for prod, c in zip(prods, targets):
            at = pl.ds(pl.multiple_of(c * BS, BS), BS)
            spread[at, :] += prod

    @pl.loop(HALF // BS, RB)
    def _(r):
        at = pl.ds(pl.multiple_of(r * BS, BS), BS)
        line = lax.broadcasted_iota(jnp.int32, (BS, F), 0) + r * BS
        outbuf[at, :] = jnp.where(line < alive, spread[at, :], F32(0.0)).astype(BF)

    top = pltpu.make_async_copy(outbuf.at[pl.ds(HALF, HALF)], input_grad.at[pl.ds(HALF, HALF)], sems.at[0])
    top.start()
    line = lax.broadcasted_iota(jnp.int32, (HALO, HALO), 0)

    flip = flips()
    lines = [pick_row(picks, k, flip) for k in range(4)]

    @pl.loop(0, HALF // HALO)
    def _(i):
        at = pl.ds(pl.multiple_of(i * HALO, HALO), HALO)
        got = spread[at, :]
        for k, r in enumerate((r0, r1, r2, r3)):
            hit = jnp.where(line + i * HALO == lines[k], F32(1.0), F32(0.0)).astype(BF)
            got = got + jnp.dot(hit, r[...], preferred_element_type=F32)
        outbuf[at, :] = got.astype(BF)
        pltpu.make_async_copy(outbuf.at[at], input_grad.at[at], sems.at[1]).start()

    low = pl.ds(0, HALF)
    pltpu.make_async_copy(outbuf.at[low], input_grad.at[low], sems.at[1]).wait()
    top.wait()


def back_part(rows, cols, count, nodes, adj, back, picks, returned):
    return pl.pallas_call(
        back_kernel,
        in_specs=[SMEM] * 4 + [HBM] * 2 + [VMEM] * 5,
        out_specs=HBM,
        out_shape=jax.ShapeDtypeStruct((NODES, F), BF),
        scratch_shapes=[
            pltpu.VMEM((BLK, BS, BS), BF),
            pltpu.VMEM((NODES, F), BF),
            pltpu.VMEM(((RB + 1) * BS, F), F32),
            pltpu.VMEM((NODES, F), BF),
            pltpu.SMEM((BLK + UNROLL,), jnp.int32),
            pltpu.SemaphoreType.DMA((4,)),
        ],
        compiler_params=pltpu.CompilerParams(vmem_limit_bytes=VMEM_BACK),
        cost_estimate=cost(12),
        name="back_part",
    )(rows, cols, count, nodes, in_hbm(adj), in_hbm(back), picks, *returned)


def exchange(parts):
    got = [None] * 4
    for k in (1, 3, 0, 2):
        axis = AXES[k // 2]
        pairs = [p for i in range(k % 2, lax.axis_size(axis) - 1, 2) for p in ((i, i + 1), (i + 1, i))]
        got[k] = lax.ppermute(parts[k], axis, pairs)
    return got


def local(features, adjacency, block_rows, block_cols, block_count, node_count, halo_index, weight, bias, out_grad):
    picks = halo_index.reshape(4, HALO)
    tables = (block_rows, block_cols, block_count, node_count)
    packed = pack(picks, features)
    packed, adjacency = lax.optimization_barrier((packed, adjacency))
    acc, adj = own_part(*tables, features, adjacency)
    halos = exchange(packed)
    output, back, r0, r1, r2, r3, terms, lines = dense_part(
        *tables, acc, adj, halos, weight, bias.reshape(1, F), out_grad
    )
    returned = exchange((r0, r1, r2, r3))
    scale = 1.0 / math.sqrt(NODES * PEERS)
    gathered = lax.all_to_all(terms, AXES, 0, 0, tiled=True).astype(F32)
    share = (jnp.sum(gathered, 0) * scale).astype(BF)
    tiles = jnp.broadcast_to(jnp.concatenate([share, lines], 0)[None], (PEERS, 24, BS))
    tiles, picks = lax.optimization_barrier((tiles, picks))
    tiles = lax.all_to_all(tiles, AXES, 0, 0, tiled=True)
    weight_grad = tiles[:, 0:16].astype(F32).reshape(64, 4, 8, BS).transpose(0, 2, 1, 3).reshape(F, F)
    sums = jnp.sum(tiles[:, 16:24].astype(F32), 0)
    bias_grad = (sums[0:4] + sums[4:8]).reshape(F) * scale
    input_grad = back_part(*tables, adjacency, back, picks, returned)
    return (output, input_grad, weight_grad, bias_grad)


def solution(mesh):
    placed = (
        P(AXES, None),
        P(AXES, None, None),
        P(AXES, None),
        P(AXES, None),
        P(AXES),
        P(AXES),
        P(AXES, None, None),
        P(),
        P(),
        P(AXES, None),
    )
    return jax.shard_map(
        local,
        mesh=mesh,
        in_specs=placed,
        out_specs=(P(AXES, None), P(AXES, None), P(), P()),
        check_vma=False,
    )
```

```python
import math

import jax
import jax.numpy as jnp
from jax import lax
from jax.experimental import pallas as pl
from jax.experimental.pallas import tpu as pltpu
from jax.sharding import PartitionSpec as P

F = 512
BS = 128
NODES = 4096
HALO = 256
RB = 32
ECB = 40
BLK = 96
HALF = 2048
CHUNK = 1024
PEERS = 128
UNROLL = 16
FEW = 8
BF = jnp.bfloat16
F32 = jnp.float32
VMEM_BYTES = 24 * 1024 * 1024
VMEM_OWN = 20 * 1024 * 1024
VMEM_DENSE = 36 * 1024 * 1024
VMEM_BACK = 20 * 1024 * 1024
VMEM_FINISH = 8 * 1024 * 1024
AXES = ("wide", "narrow")


SMEM = pl.BlockSpec(memory_space=pltpu.SMEM)
VMEM = pl.BlockSpec(memory_space=pltpu.VMEM)
HBM = pl.BlockSpec(memory_space=pl.ANY)


def cost(us):
    return pl.CostEstimate(flops=int(us * 1e9), bytes_accessed=int(us * 3e6), transcendentals=0)


def held(x):
    return pltpu.with_memory_space_constraint(x, pltpu.VMEM)


def in_hbm(x):
    return pltpu.with_memory_space_constraint(x, pltpu.HBM)


def flips():
    return 1 - (lax.axis_index("wide") & 1), 1 - (lax.axis_index("narrow") & 1)


def pick_row(picks, k, flip):
    return picks[pl.ds((k & 2) + ((k & 1) ^ flip[k // 2]), 1), :]


def pack_kernel(picks, feats_in, out0, out1, out2, out3, onehot, feats, sem):
    outs = (out0, out1, out2, out3)
    load = pltpu.make_async_copy(feats_in.at[pl.ds(0, HALF)], feats, sem.at[0])
    load.start()
    lane = lax.broadcasted_iota(jnp.int32, (BS, BS), 1)

    flip = flips()

    def build(k):
        line = pick_row(picks, k, flip)
        for h in range(2):
            row = line[:, h * BS : (h + 1) * BS]
            t = jnp.transpose(jnp.broadcast_to(row.astype(F32), (BS, BS))).astype(jnp.int32)
            for c in range(HALF // BS):
                hit = jnp.where(t == lane + c * BS, F32(1.0), F32(0.0)).astype(BF)
                onehot[k * HALO + h * BS : k * HALO + (h + 1) * BS, c * BS : (c + 1) * BS] = hit

    build(0)
    build(1)
    load.wait()
    for k in range(4):
        if k >= 2:
            build(k)
        outs[k][...] = jnp.dot(onehot[k * HALO : (k + 1) * HALO, :], feats[...], preferred_element_type=F32).astype(BF)


def pack(picks, features):
    return pl.pallas_call(
        pack_kernel,
        in_specs=[VMEM, HBM],
        out_specs=[VMEM] * 4,
        out_shape=[jax.ShapeDtypeStruct((HALO, F), BF)] * 4,
        scratch_shapes=[
            pltpu.VMEM((4 * HALO, HALF), BF),
            pltpu.VMEM((HALF, F), BF),
            pltpu.SemaphoreType.DMA((1,)),
        ],
        compiler_params=pltpu.CompilerParams(vmem_limit_bytes=VMEM_BYTES),
        cost_estimate=cost(3),
        name="pack",
    )(picks, in_hbm(features))


def block(ref, i):
    return ref[pl.ds(pl.multiple_of(i * BS, BS), BS), :]


def tail_mask(ref, start, alive):
    @pl.loop(start, RB)
    def _(r):
        at = pl.ds(pl.multiple_of(r * BS, BS), BS)
        line = lax.broadcasted_iota(jnp.int32, (BS, F), 0) + r * BS
        ref[at, :] = jnp.where(line < alive, ref[at, :].astype(F32), F32(0.0)).astype(BF)


def zero_blocks(ref, count):
    @pl.loop(0, count)
    def _(r):
        ref[pl.ds(pl.multiple_of(r * BS, BS), BS), :] = jnp.zeros((BS, F), F32)


def slot_list(table, rows, cols, live, halo, spare, unroll):
    flip = flips()

    def step(b, n):
        c = cols[0, b]
        take = jnp.logical_and(b < live, (c >= RB) == (halo == 1))
        turn = jnp.where(c < RB, 0, jnp.where(c < RB + 4, flip[0], flip[1]) * 2)
        table[n] = b + (rows[0, b] << 8) + ((c ^ turn) << 16)
        return n + take.astype(jnp.int32)

    n = lax.fori_loop(0, BLK, step, jnp.int32(0))
    for u in range(unroll):
        table[n + u] = jnp.int32(spare)
    return (n + unroll - 1) // unroll


def unpack(code):
    return code & 255, (code >> 8) & 255, code >> 16


def own_kernel(rows, cols, count, nodes, feats, adj_in, acc, adj, ext, table, sems):
    loads = [
        pltpu.make_async_copy(adj_in, adj, sems.at[0]),
        pltpu.make_async_copy(feats, ext, sems.at[1]),
    ]
    for c in loads:
        c.start()
    zero_blocks(acc, RB + 1)
    groups = slot_list(table, rows, cols, count[0], 0, RB << 8, UNROLL)
    for c in loads:
        c.wait()
    tail_mask(ext, nodes[0] // BS, nodes[0])

    @pl.loop(0, groups)
    def _(i):
        prods, targets = [], []
        for u in range(UNROLL):
            b, r, c = unpack(table[i * UNROLL + u])
            prods.append(jnp.dot(adj[b], block(ext, c), preferred_element_type=F32))
            targets.append(r)
        for prod, r in zip(prods, targets):
            at = pl.ds(pl.multiple_of(r * BS, BS), BS)
            acc[at, :] += prod


def own_part(rows, cols, count, nodes, features, adjacency):
    return pl.pallas_call(
        own_kernel,
        in_specs=[SMEM] * 4 + [HBM] * 2,
        out_specs=[VMEM] * 2,
        out_shape=[pltpu.VMEM(((RB + 1) * BS, F), F32), pltpu.VMEM((BLK, BS, BS), BF)],
        scratch_shapes=[
            pltpu.VMEM((NODES, F), BF),
            pltpu.SMEM((BLK + UNROLL,), jnp.int32),
            pltpu.SemaphoreType.DMA((2,)),
        ],
        compiler_params=pltpu.CompilerParams(vmem_limit_bytes=VMEM_OWN),
        cost_estimate=cost(8),
        name="own_part",
    )(rows, cols, count, nodes, in_hbm(features), in_hbm(adjacency))


def dense_kernel(
    rows, cols, count, nodes, acc_in, adj, h0, h1, h2, h3, weight, bias, grads_in,
    acc, output, back_out, ret0, ret1, ret2, ret3, terms, lines_out,
    back, received, spread, grads, outbuf, wacc, bacc, table, gsems, osems,
):
    alive = nodes[0]
    halos = (h0, h1, h2, h3)

    def grad_copy(i):
        at = pl.ds(pl.multiple_of(i * CHUNK, CHUNK), CHUNK)
        return pltpu.make_async_copy(grads_in.at[at], grads.at[at], gsems.at[i])

    for i in range(NODES // CHUNK):
        grad_copy(i).start()
    groups = slot_list(table, rows, cols, count[0], 1, (RB << 8) + (ECB << 16), FEW)
    zero_blocks(spread, ECB - RB + 1)
    wacc[...] = jnp.zeros_like(wacc)
    bacc[...] = jnp.zeros_like(bacc)
    for k in range(4):
        hal_at = pl.ds(k * HALO, HALO)
        received[hal_at, :] = halos[k][...]

    @pl.loop(0, groups)
    def _(i):
        prods, targets = [], []
        for u in range(FEW):
            b, r, c = unpack(table[i * FEW + u])
            prods.append(jnp.dot(adj[b], block(received, c - RB), preferred_element_type=F32))
            targets.append(r)
        for prod, r in zip(prods, targets):
            at = pl.ds(pl.multiple_of(r * BS, BS), BS)
            acc[at, :] += prod

    @pl.loop(0, NODES // CHUNK)
    def _(i):
        base = pl.multiple_of(i * CHUNK, CHUNK)
        at = pl.ds(base, CHUNK)
        grad_copy(i).wait()
        agg = acc[at, :].astype(BF)
        pre = jnp.dot(agg, weight[...], preferred_element_type=F32) + bias[...]
        sig = jax.nn.sigmoid(pre)
        keep = lax.broadcasted_iota(jnp.int32, (CHUNK, F), 0) + base < alive
        outbuf[at, :] = jnp.where(keep, pre * sig, F32(0.0)).astype(BF)
        pltpu.make_async_copy(outbuf.at[at], output.at[at], osems.at[0]).start()
        g = grads[at, :].astype(F32)
        dpre = jnp.where(keep, g * sig * (1.0 + pre * (1.0 - sig)), F32(0.0)).astype(BF)
        bacc[...] += jnp.sum(dpre.astype(F32).reshape(CHUNK // 8, 8, F), 0)
        wacc[...] += lax.dot_general(agg, dpre, (((0,), (0,)), ((), ())), preferred_element_type=F32)
        back[at, :] = lax.dot_general(
            dpre, weight[...], (((1,), (1,)), ((), ())), preferred_element_type=F32
        ).astype(BF)
        pltpu.make_async_copy(back.at[at], back_out.at[at], osems.at[1]).start()

    for p in range(PEERS):
        for t in range(2):
            a, c = p // 2, p % 2 * 2 + t
            terms[p, 8 * t : 8 * t + 8, :] = wacc[a * 8 : (a + 1) * 8, c * BS : (c + 1) * BS].astype(BF)
    total = jnp.sum(bacc[...], 0, keepdims=True)
    high = total.astype(BF).astype(F32)
    low = total - high
    lines = jnp.concatenate(
        [high[:, c * BS : (c + 1) * BS] for c in range(4)] + [low[:, c * BS : (c + 1) * BS] for c in range(4)], 0
    ).astype(BF)
    lines_out[...] = lines

    @pl.loop(0, groups)
    def _(i):
        prods, targets = [], []
        for u in range(FEW):
            b, r, c = unpack(table[i * FEW + u])
            r = jnp.where(r < RB, r, 0)
            prods.append(
                lax.dot_general(adj[b], block(back, r), (((0,), (0,)), ((), ())), preferred_element_type=F32)
            )
            targets.append(c - RB)
        for prod, c in zip(prods, targets):
            at = pl.ds(pl.multiple_of(c * BS, BS), BS)
            spread[at, :] += prod

    for k, ret in enumerate((ret0, ret1, ret2, ret3)):
        ret[...] = spread[k * HALO : (k + 1) * HALO, :].astype(BF)
    pltpu.make_async_copy(outbuf, output, osems.at[0]).wait()
    pltpu.make_async_copy(back, back_out, osems.at[1]).wait()


def dense_part(rows, cols, count, nodes, acc, adj, halos, weight, bias, out_grad):
    return pl.pallas_call(
        dense_kernel,
        in_specs=[SMEM] * 4 + [VMEM] * 8 + [HBM],
        out_specs=[VMEM, HBM, HBM] + [VMEM] * 6,
        out_shape=[
            pltpu.VMEM(((RB + 1) * BS, F), F32),
            jax.ShapeDtypeStruct((NODES, F), BF),
            jax.ShapeDtypeStruct((NODES, F), BF),
        ]
        + [jax.ShapeDtypeStruct((HALO, F), BF)] * 4
        + [jax.ShapeDtypeStruct((PEERS, 16, BS), BF), jax.ShapeDtypeStruct((8, BS), BF)],
        input_output_aliases={4: 0},
        scratch_shapes=[
            pltpu.VMEM((NODES, F), BF),
            pltpu.VMEM(((ECB - RB + 1) * BS, F), BF),
            pltpu.VMEM(((ECB - RB + 1) * BS, F), F32),
            pltpu.VMEM((NODES, F), BF),
            pltpu.VMEM((NODES, F), BF),
            pltpu.VMEM((F, F), F32),
            pltpu.VMEM((8, F), F32),
            pltpu.SMEM((BLK + UNROLL,), jnp.int32),
            pltpu.SemaphoreType.DMA((NODES // CHUNK,)),
            pltpu.SemaphoreType.DMA((2,)),
        ],
        compiler_params=pltpu.CompilerParams(vmem_limit_bytes=VMEM_DENSE),
        cost_estimate=cost(16),
        name="dense_part",
    )(rows, cols, count, nodes, held(acc), held(adj), *halos, weight, bias, in_hbm(out_grad))[1:]


def back_kernel(
    rows, cols, count, nodes, adj_in, back_in, spread, input_grad, adj, back, outbuf, table, sems
):
    alive = nodes[0]
    loads = [
        pltpu.make_async_copy(adj_in, adj, sems.at[1]),
        pltpu.make_async_copy(back_in, back, sems.at[2]),
    ]
    for c in loads:
        c.start()
    zero_blocks(spread, RB + 1)
    groups = slot_list(table, rows, cols, count[0], 0, RB << 16, UNROLL)
    for c in loads:
        c.wait()

    @pl.loop(0, groups)
    def _(i):
        prods, targets = [], []
        for u in range(UNROLL):
            b, r, c = unpack(table[i * UNROLL + u])
            prods.append(
                lax.dot_general(adj[b], block(back, r), (((0,), (0,)), ((), ())), preferred_element_type=F32)
            )
            targets.append(c)
        for prod, c in zip(prods, targets):
            at = pl.ds(pl.multiple_of(c * BS, BS), BS)
            spread[at, :] += prod

    @pl.loop(HALF // BS, RB)
    def _(r):
        at = pl.ds(pl.multiple_of(r * BS, BS), BS)
        to = pl.ds(pl.multiple_of(r * BS - HALF, BS), BS)
        line = lax.broadcasted_iota(jnp.int32, (BS, F), 0) + r * BS
        outbuf[to, :] = jnp.where(line < alive, spread[at, :], F32(0.0)).astype(BF)

    top = pltpu.make_async_copy(outbuf, input_grad.at[pl.ds(HALF, HALF)], sems.at[0])
    top.start()
    top.wait()


def back_part(rows, cols, count, nodes, adj, back):
    return pl.pallas_call(
        back_kernel,
        in_specs=[SMEM] * 4 + [HBM] * 2,
        out_specs=[VMEM, HBM],
        out_shape=[pltpu.VMEM(((RB + 1) * BS, F), F32), jax.ShapeDtypeStruct((NODES, F), BF)],
        scratch_shapes=[
            pltpu.VMEM((BLK, BS, BS), BF),
            pltpu.VMEM((NODES, F), BF),
            pltpu.VMEM((HALF, F), BF),
            pltpu.SMEM((BLK + UNROLL,), jnp.int32),
            pltpu.SemaphoreType.DMA((3,)),
        ],
        compiler_params=pltpu.CompilerParams(vmem_limit_bytes=VMEM_BACK),
        cost_estimate=cost(9),
        name="back_part",
    )(rows, cols, count, nodes, in_hbm(adj), in_hbm(back))


def finish_kernel(picks, spread, r0, r1, r2, r3, partial, input_grad, outbuf, sems):
    line = lax.broadcasted_iota(jnp.int32, (HALO, HALO), 0)
    flip = flips()
    lines = [pick_row(picks, k, flip) for k in range(4)]

    @pl.loop(0, HALF // HALO)
    def _(i):
        at = pl.ds(pl.multiple_of(i * HALO, HALO), HALO)
        got = spread[at, :]
        for k, r in enumerate((r0, r1, r2, r3)):
            hit = jnp.where(line + i * HALO == lines[k], F32(1.0), F32(0.0)).astype(BF)
            got = got + jnp.dot(hit, r[...], preferred_element_type=F32)
        outbuf[at, :] = got.astype(BF)
        pltpu.make_async_copy(outbuf.at[at], input_grad.at[at], sems.at[0]).start()

    pltpu.make_async_copy(outbuf, input_grad.at[pl.ds(0, HALF)], sems.at[0]).wait()


def finish(picks, spread, returned, input_grad):
    return pl.pallas_call(
        finish_kernel,
        in_specs=[VMEM] * 6 + [HBM],
        out_specs=HBM,
        out_shape=jax.ShapeDtypeStruct((NODES, F), BF),
        input_output_aliases={6: 0},
        scratch_shapes=[pltpu.VMEM((HALF, F), BF), pltpu.SemaphoreType.DMA((1,))],
        compiler_params=pltpu.CompilerParams(vmem_limit_bytes=VMEM_FINISH),
        cost_estimate=cost(4),
        name="finish",
    )(picks, held(spread), *returned, input_grad)


def exchange(parts):
    got = [None] * 4
    for k in (1, 3, 0, 2):
        axis = AXES[k // 2]
        pairs = [p for i in range(k % 2, lax.axis_size(axis) - 1, 2) for p in ((i, i + 1), (i + 1, i))]
        got[k] = lax.ppermute(parts[k], axis, pairs)
    return got


def local(features, adjacency, block_rows, block_cols, block_count, node_count, halo_index, weight, bias, out_grad):
    picks = halo_index.reshape(4, HALO)
    tables = (block_rows, block_cols, block_count, node_count)
    packed = pack(picks, features)
    packed, adjacency = lax.optimization_barrier((packed, adjacency))
    acc, adj = own_part(*tables, features, adjacency)
    halos = exchange(packed)
    output, back, r0, r1, r2, r3, terms, lines = dense_part(
        *tables, acc, adj, halos, weight, bias.reshape(1, F), out_grad
    )
    returned = exchange((r0, r1, r2, r3))
    scale = 1.0 / math.sqrt(NODES * PEERS)
    gathered = lax.all_to_all(terms, AXES, 0, 0, tiled=True).astype(F32)
    share = (jnp.sum(gathered, 0) * scale).astype(BF)
    tiles = jnp.broadcast_to(jnp.concatenate([share, lines], 0)[None], (PEERS, 24, BS))
    tiles, adjacency = lax.optimization_barrier((tiles, adjacency))
    tiles = lax.all_to_all(tiles, AXES, 0, 0, tiled=True)
    weight_grad = tiles[:, 0:16].astype(F32).reshape(64, 4, 8, BS).transpose(0, 2, 1, 3).reshape(F, F)
    sums = jnp.sum(tiles[:, 16:24].astype(F32), 0)
    bias_grad = (sums[0:4] + sums[4:8]).reshape(F) * scale
    spread, partial_grad = back_part(*tables, adjacency, back)
    input_grad = finish(picks, spread, returned, partial_grad)
    return (output, input_grad, weight_grad, bias_grad)


def solution(mesh):
    placed = (
        P(AXES, None),
        P(AXES, None, None),
        P(AXES, None),
        P(AXES, None),
        P(AXES),
        P(AXES),
        P(AXES, None, None),
        P(),
        P(),
        P(AXES, None),
    )
    return jax.shard_map(
        local,
        mesh=mesh,
        in_specs=placed,
        out_specs=(P(AXES, None), P(AXES, None), P(), P()),
        check_vma=False,
    )
```

```python
import math

import jax
import jax.numpy as jnp
from jax import lax
from jax.experimental import pallas as pl
from jax.experimental.pallas import tpu as pltpu
from jax.sharding import PartitionSpec as P

F = 512
BS = 128
NODES = 4096
HALO = 256
RB = 32
ECB = 40
BLK = 96
HALF = 2048
CHUNK = 1024
DEVICES = 128
PEERS = 64
UNROLL = 16
FEW = 8
BF = jnp.bfloat16
F32 = jnp.float32
VMEM_BYTES = 24 * 1024 * 1024
VMEM_OWN = 20 * 1024 * 1024
VMEM_DENSE = 36 * 1024 * 1024
VMEM_BACK = 20 * 1024 * 1024
VMEM_FINISH = 8 * 1024 * 1024
WIDE = ("far", "core")
AXES = ("far", "core", "narrow")
CHIPS = ("far", "narrow")
SIDES = (WIDE, "narrow")


SMEM = pl.BlockSpec(memory_space=pltpu.SMEM)
VMEM = pl.BlockSpec(memory_space=pltpu.VMEM)
HBM = pl.BlockSpec(memory_space=pl.ANY)


def cost(us):
    return pl.CostEstimate(flops=int(us * 1e9), bytes_accessed=int(us * 3e6), transcendentals=0)


def held(x):
    return pltpu.with_memory_space_constraint(x, pltpu.VMEM)


def in_hbm(x):
    return pltpu.with_memory_space_constraint(x, pltpu.HBM)


def flips():
    return 1 - lax.axis_index("core"), 1 - (lax.axis_index("narrow") & 1)


def pick_row(picks, k, flip):
    return picks[pl.ds((k & 2) + ((k & 1) ^ flip[k // 2]), 1), :]


def pack_kernel(picks, feats_in, out0, out1, out2, out3, onehot, feats, sem):
    outs = (out0, out1, out2, out3)
    load = pltpu.make_async_copy(feats_in.at[pl.ds(0, HALF)], feats, sem.at[0])
    load.start()
    lane = lax.broadcasted_iota(jnp.int32, (BS, BS), 1)

    flip = flips()

    def build(k):
        line = pick_row(picks, k, flip)
        for h in range(2):
            row = line[:, h * BS : (h + 1) * BS]
            t = jnp.transpose(jnp.broadcast_to(row.astype(F32), (BS, BS))).astype(jnp.int32)
            for c in range(HALF // BS):
                hit = jnp.where(t == lane + c * BS, F32(1.0), F32(0.0)).astype(BF)
                onehot[k * HALO + h * BS : k * HALO + (h + 1) * BS, c * BS : (c + 1) * BS] = hit

    build(0)
    build(1)
    load.wait()
    for k in range(4):
        if k >= 2:
            build(k)
        outs[k][...] = jnp.dot(onehot[k * HALO : (k + 1) * HALO, :], feats[...], preferred_element_type=F32).astype(BF)


def pack(picks, features):
    return pl.pallas_call(
        pack_kernel,
        in_specs=[VMEM, HBM],
        out_specs=[VMEM] * 4,
        out_shape=[jax.ShapeDtypeStruct((HALO, F), BF)] * 4,
        scratch_shapes=[
            pltpu.VMEM((4 * HALO, HALF), BF),
            pltpu.VMEM((HALF, F), BF),
            pltpu.SemaphoreType.DMA((1,)),
        ],
        compiler_params=pltpu.CompilerParams(vmem_limit_bytes=VMEM_BYTES),
        cost_estimate=cost(3),
        name="pack",
    )(picks, in_hbm(features))


def block(ref, i):
    return ref[pl.ds(pl.multiple_of(i * BS, BS), BS), :]


def tail_mask(ref, start, alive):
    @pl.loop(start, RB)
    def _(r):
        at = pl.ds(pl.multiple_of(r * BS, BS), BS)
        line = lax.broadcasted_iota(jnp.int32, (BS, F), 0) + r * BS
        ref[at, :] = jnp.where(line < alive, ref[at, :].astype(F32), F32(0.0)).astype(BF)


def zero_blocks(ref, count):
    @pl.loop(0, count)
    def _(r):
        ref[pl.ds(pl.multiple_of(r * BS, BS), BS), :] = jnp.zeros((BS, F), F32)


def slot_list(table, rows, cols, live, halo, spare, unroll):
    flip = flips()

    def step(b, n):
        c = cols[0, b]
        take = jnp.logical_and(b < live, (c >= RB) == (halo == 1))
        turn = jnp.where(c < RB, 0, jnp.where(c < RB + 4, flip[0], flip[1]) * 2)
        table[n] = b + (rows[0, b] << 8) + ((c ^ turn) << 16)
        return n + take.astype(jnp.int32)

    n = lax.fori_loop(0, BLK, step, jnp.int32(0))
    for u in range(unroll):
        table[n + u] = jnp.int32(spare)
    return (n + unroll - 1) // unroll


def unpack(code):
    return code & 255, (code >> 8) & 255, code >> 16


def own_kernel(rows, cols, count, nodes, feats, adj_in, acc, adj, ext, table, sems):
    loads = [
        pltpu.make_async_copy(adj_in, adj, sems.at[0]),
        pltpu.make_async_copy(feats, ext, sems.at[1]),
    ]
    for c in loads:
        c.start()
    zero_blocks(acc, RB + 1)
    groups = slot_list(table, rows, cols, count[0], 0, RB << 8, UNROLL)
    for c in loads:
        c.wait()
    tail_mask(ext, nodes[0] // BS, nodes[0])

    @pl.loop(0, groups)
    def _(i):
        prods, targets = [], []
        for u in range(UNROLL):
            b, r, c = unpack(table[i * UNROLL + u])
            prods.append(jnp.dot(adj[b], block(ext, c), preferred_element_type=F32))
            targets.append(r)
        for prod, r in zip(prods, targets):
            at = pl.ds(pl.multiple_of(r * BS, BS), BS)
            acc[at, :] += prod


def own_part(rows, cols, count, nodes, features, adjacency):
    return pl.pallas_call(
        own_kernel,
        in_specs=[SMEM] * 4 + [HBM] * 2,
        out_specs=[VMEM] * 2,
        out_shape=[pltpu.VMEM(((RB + 1) * BS, F), F32), pltpu.VMEM((BLK, BS, BS), BF)],
        scratch_shapes=[
            pltpu.VMEM((NODES, F), BF),
            pltpu.SMEM((BLK + UNROLL,), jnp.int32),
            pltpu.SemaphoreType.DMA((2,)),
        ],
        compiler_params=pltpu.CompilerParams(vmem_limit_bytes=VMEM_OWN),
        cost_estimate=cost(8),
        name="own_part",
    )(rows, cols, count, nodes, in_hbm(features), in_hbm(adjacency))


def dense_kernel(
    rows, cols, count, nodes, acc_in, adj, h0, h1, h2, h3, weight, bias, grads_in,
    acc, output, back_out, ret0, ret1, ret2, ret3, mine, give, lines_out,
    back, received, spread, grads, outbuf, wacc, bacc, table, gsems, osems,
):
    alive = nodes[0]
    halos = (h0, h1, h2, h3)

    def grad_copy(i):
        at = pl.ds(pl.multiple_of(i * CHUNK, CHUNK), CHUNK)
        return pltpu.make_async_copy(grads_in.at[at], grads.at[at], gsems.at[i])

    for i in range(NODES // CHUNK):
        grad_copy(i).start()
    groups = slot_list(table, rows, cols, count[0], 1, (RB << 8) + (ECB << 16), FEW)
    zero_blocks(spread, ECB - RB + 1)
    wacc[...] = jnp.zeros_like(wacc)
    bacc[...] = jnp.zeros_like(bacc)
    for k in range(4):
        hal_at = pl.ds(k * HALO, HALO)
        received[hal_at, :] = halos[k][...]

    @pl.loop(0, groups)
    def _(i):
        prods, targets = [], []
        for u in range(FEW):
            b, r, c = unpack(table[i * FEW + u])
            prods.append(jnp.dot(adj[b], block(received, c - RB), preferred_element_type=F32))
            targets.append(r)
        for prod, r in zip(prods, targets):
            at = pl.ds(pl.multiple_of(r * BS, BS), BS)
            acc[at, :] += prod

    @pl.loop(0, NODES // CHUNK)
    def _(i):
        base = pl.multiple_of(i * CHUNK, CHUNK)
        at = pl.ds(base, CHUNK)
        grad_copy(i).wait()
        agg = acc[at, :].astype(BF)
        pre = jnp.dot(agg, weight[...], preferred_element_type=F32) + bias[...]
        sig = jax.nn.sigmoid(pre)
        keep = lax.broadcasted_iota(jnp.int32, (CHUNK, F), 0) + base < alive
        outbuf[at, :] = jnp.where(keep, pre * sig, F32(0.0)).astype(BF)
        pltpu.make_async_copy(outbuf.at[at], output.at[at], osems.at[0]).start()
        g = grads[at, :].astype(F32)
        dpre = jnp.where(keep, g * sig * (1.0 + pre * (1.0 - sig)), F32(0.0)).astype(BF)
        bacc[...] += jnp.sum(dpre.astype(F32).reshape(CHUNK // 8, 8, F), 0)
        wacc[...] += lax.dot_general(agg, dpre, (((0,), (0,)), ((), ())), preferred_element_type=F32)
        back[at, :] = lax.dot_general(
            dpre, weight[...], (((1,), (1,)), ((), ())), preferred_element_type=F32
        ).astype(BF)
        pltpu.make_async_copy(back.at[at], back_out.at[at], osems.at[1]).start()

    core = lax.axis_index("core")
    for out, half, kind in ((mine, core, F32), (give, 1 - core, BF)):
        for p in range(PEERS):
            for t in range(2):
                a, c = p // 2, p % 2 * 2 + t
                tile = wacc[pl.ds(pl.multiple_of(half * (F // 2) + a * 8, 8), 8), c * BS : (c + 1) * BS]
                out[p, 8 * t : 8 * t + 8, :] = tile.astype(kind)
    total = jnp.sum(bacc[...], 0, keepdims=True)
    high = total.astype(BF).astype(F32)
    low = total - high
    lines = jnp.concatenate(
        [high[:, c * BS : (c + 1) * BS] for c in range(4)] + [low[:, c * BS : (c + 1) * BS] for c in range(4)], 0
    ).astype(BF)
    lines_out[...] = lines
    give[PEERS] = jnp.concatenate([lines, lines], 0)

    @pl.loop(0, groups)
    def _(i):
        prods, targets = [], []
        for u in range(FEW):
            b, r, c = unpack(table[i * FEW + u])
            r = jnp.where(r < RB, r, 0)
            prods.append(
                lax.dot_general(adj[b], block(back, r), (((0,), (0,)), ((), ())), preferred_element_type=F32)
            )
            targets.append(c - RB)
        for prod, c in zip(prods, targets):
            at = pl.ds(pl.multiple_of(c * BS, BS), BS)
            spread[at, :] += prod

    for k, ret in enumerate((ret0, ret1, ret2, ret3)):
        ret[...] = spread[k * HALO : (k + 1) * HALO, :].astype(BF)
    pltpu.make_async_copy(outbuf, output, osems.at[0]).wait()
    pltpu.make_async_copy(back, back_out, osems.at[1]).wait()


def dense_part(rows, cols, count, nodes, acc, adj, halos, weight, bias, out_grad):
    return pl.pallas_call(
        dense_kernel,
        in_specs=[SMEM] * 4 + [VMEM] * 8 + [HBM],
        out_specs=[VMEM, HBM, HBM] + [VMEM] * 7,
        out_shape=[
            pltpu.VMEM(((RB + 1) * BS, F), F32),
            jax.ShapeDtypeStruct((NODES, F), BF),
            jax.ShapeDtypeStruct((NODES, F), BF),
        ]
        + [jax.ShapeDtypeStruct((HALO, F), BF)] * 4
        + [jax.ShapeDtypeStruct((PEERS, 16, BS), F32),
            jax.ShapeDtypeStruct((PEERS + 1, 16, BS), BF),
            jax.ShapeDtypeStruct((8, BS), BF),
        ],
        input_output_aliases={4: 0},
        scratch_shapes=[
            pltpu.VMEM((NODES, F), BF),
            pltpu.VMEM(((ECB - RB + 1) * BS, F), BF),
            pltpu.VMEM(((ECB - RB + 1) * BS, F), F32),
            pltpu.VMEM((NODES, F), BF),
            pltpu.VMEM((NODES, F), BF),
            pltpu.VMEM((F, F), F32),
            pltpu.VMEM((8, F), F32),
            pltpu.SMEM((BLK + UNROLL,), jnp.int32),
            pltpu.SemaphoreType.DMA((NODES // CHUNK,)),
            pltpu.SemaphoreType.DMA((2,)),
        ],
        compiler_params=pltpu.CompilerParams(vmem_limit_bytes=VMEM_DENSE),
        cost_estimate=cost(16),
        name="dense_part",
    )(rows, cols, count, nodes, held(acc), held(adj), *halos, weight, bias, in_hbm(out_grad))[1:]


def back_kernel(
    rows, cols, count, nodes, adj_in, back_in, spread, input_grad, adj, back, outbuf, table, sems
):
    alive = nodes[0]
    loads = [
        pltpu.make_async_copy(adj_in, adj, sems.at[1]),
        pltpu.make_async_copy(back_in, back, sems.at[2]),
    ]
    for c in loads:
        c.start()
    zero_blocks(spread, RB + 1)
    groups = slot_list(table, rows, cols, count[0], 0, RB << 16, UNROLL)
    for c in loads:
        c.wait()

    @pl.loop(0, groups)
    def _(i):
        prods, targets = [], []
        for u in range(UNROLL):
            b, r, c = unpack(table[i * UNROLL + u])
            prods.append(
                lax.dot_general(adj[b], block(back, r), (((0,), (0,)), ((), ())), preferred_element_type=F32)
            )
            targets.append(c)
        for prod, c in zip(prods, targets):
            at = pl.ds(pl.multiple_of(c * BS, BS), BS)
            spread[at, :] += prod

    @pl.loop(HALF // BS, RB)
    def _(r):
        at = pl.ds(pl.multiple_of(r * BS, BS), BS)
        to = pl.ds(pl.multiple_of(r * BS - HALF, BS), BS)
        line = lax.broadcasted_iota(jnp.int32, (BS, F), 0) + r * BS
        outbuf[to, :] = jnp.where(line < alive, spread[at, :], F32(0.0)).astype(BF)

    top = pltpu.make_async_copy(outbuf, input_grad.at[pl.ds(HALF, HALF)], sems.at[0])
    top.start()
    top.wait()


def back_part(rows, cols, count, nodes, adj, back):
    return pl.pallas_call(
        back_kernel,
        in_specs=[SMEM] * 4 + [HBM] * 2,
        out_specs=[VMEM, HBM],
        out_shape=[pltpu.VMEM(((RB + 1) * BS, F), F32), jax.ShapeDtypeStruct((NODES, F), BF)],
        scratch_shapes=[
            pltpu.VMEM((BLK, BS, BS), BF),
            pltpu.VMEM((NODES, F), BF),
            pltpu.VMEM((HALF, F), BF),
            pltpu.SMEM((BLK + UNROLL,), jnp.int32),
            pltpu.SemaphoreType.DMA((3,)),
        ],
        compiler_params=pltpu.CompilerParams(vmem_limit_bytes=VMEM_BACK),
        cost_estimate=cost(9),
        name="back_part",
    )(rows, cols, count, nodes, in_hbm(adj), in_hbm(back))


def finish_kernel(picks, spread, r0, r1, r2, r3, partial, input_grad, outbuf, sems):
    line = lax.broadcasted_iota(jnp.int32, (HALO, HALO), 0)
    flip = flips()
    lines = [pick_row(picks, k, flip) for k in range(4)]

    @pl.loop(0, HALF // HALO)
    def _(i):
        at = pl.ds(pl.multiple_of(i * HALO, HALO), HALO)
        got = spread[at, :]
        for k, r in enumerate((r0, r1, r2, r3)):
            hit = jnp.where(line + i * HALO == lines[k], F32(1.0), F32(0.0)).astype(BF)
            got = got + jnp.dot(hit, r[...], preferred_element_type=F32)
        outbuf[at, :] = got.astype(BF)
        pltpu.make_async_copy(outbuf.at[at], input_grad.at[at], sems.at[0]).start()

    pltpu.make_async_copy(outbuf, input_grad.at[pl.ds(0, HALF)], sems.at[0]).wait()


def finish(picks, spread, returned, input_grad):
    return pl.pallas_call(
        finish_kernel,
        in_specs=[VMEM] * 6 + [HBM],
        out_specs=HBM,
        out_shape=jax.ShapeDtypeStruct((NODES, F), BF),
        input_output_aliases={6: 0},
        scratch_shapes=[pltpu.VMEM((HALF, F), BF), pltpu.SemaphoreType.DMA((1,))],
        compiler_params=pltpu.CompilerParams(vmem_limit_bytes=VMEM_FINISH),
        cost_estimate=cost(4),
        name="finish",
    )(picks, held(spread), *returned, input_grad)


def pair_kernel(mine, given, lines, pair, both_lines):
    pair[...] = (mine[...] + given[0:PEERS].astype(F32)).astype(BF)
    near, far = lines[...].astype(F32), given[PEERS, 0:8, :].astype(F32)
    both = near[0:4] + near[4:8] + (far[0:4] + far[4:8])
    high = both.astype(BF).astype(F32)
    both_lines[...] = jnp.concatenate([high, both - high], 0).astype(BF)


def pair_sum(mine, given, lines):
    return pl.pallas_call(
        pair_kernel,
        in_specs=[VMEM] * 3,
        out_specs=[VMEM] * 2,
        out_shape=[jax.ShapeDtypeStruct((PEERS, 16, BS), BF), jax.ShapeDtypeStruct((8, BS), BF)],
        compiler_params=pltpu.CompilerParams(vmem_limit_bytes=VMEM_FINISH),
        cost_estimate=cost(1),
        name="pair_sum",
    )(mine, given, lines)


def join_kernel(tiles, other, weight_grad, bias_grad):
    core = lax.axis_index("core")
    for half, src in ((core, tiles), (1 - core, other)):
        for p in range(PEERS):
            for t in range(2):
                a, c = p // 2, p % 2 * 2 + t
                at = pl.ds(pl.multiple_of(half * (F // 2) + a * 8, 8), 8)
                weight_grad[at, c * BS : (c + 1) * BS] = src[p, 8 * t : 8 * t + 8, :].astype(F32)
    sums = jnp.sum(tiles[:, 16:24, :].astype(F32), 0)
    bias_grad[...] = (sums[0:4] + sums[4:8]) * (1.0 / math.sqrt(NODES * DEVICES))


def join(tiles, other):
    return pl.pallas_call(
        join_kernel,
        in_specs=[VMEM] * 2,
        out_specs=[VMEM] * 2,
        out_shape=[jax.ShapeDtypeStruct((F, F), F32), jax.ShapeDtypeStruct((F // BS, BS), F32)],
        compiler_params=pltpu.CompilerParams(vmem_limit_bytes=VMEM_FINISH),
        cost_estimate=cost(1),
        name="join",
    )(tiles, other)


def exchange(parts):
    got = [None] * 4
    for k in (1, 3, 0, 2):
        axis = SIDES[k // 2]
        pairs = [p for i in range(k % 2, lax.axis_size(axis) - 1, 2) for p in ((i, i + 1), (i + 1, i))]
        got[k] = lax.ppermute(parts[k], axis, pairs)
    return got


def local(features, adjacency, block_rows, block_cols, block_count, node_count, halo_index, weight, bias, out_grad):
    picks = halo_index.reshape(4, HALO)
    tables = (block_rows, block_cols, block_count, node_count)
    packed = pack(picks, features)
    packed, adjacency = lax.optimization_barrier((packed, adjacency))
    acc, adj = own_part(*tables, features, adjacency)
    halos = exchange(packed)
    output, back, r0, r1, r2, r3, mine, give, lines = dense_part(
        *tables, acc, adj, halos, weight, bias.reshape(1, F), out_grad
    )
    scale = 1.0 / math.sqrt(NODES * DEVICES)
    swap = [(0, 1), (1, 0)]
    pair, lines = pair_sum(mine, lax.ppermute(give, "core", swap), lines)
    pair, r0, r1, r2, r3 = lax.optimization_barrier((pair, r0, r1, r2, r3))
    returned = exchange((r0, r1, r2, r3))
    gathered = lax.all_to_all(pair, CHIPS, 0, 0, tiled=True).astype(F32)
    share = (jnp.sum(gathered, 0) * scale).astype(BF)
    tiles = jnp.broadcast_to(jnp.concatenate([share, lines], 0)[None], (PEERS, 24, BS))
    tiles, adjacency = lax.optimization_barrier((tiles, adjacency))
    tiles = lax.all_to_all(tiles, CHIPS, 0, 0, tiled=True)
    spread, partial_grad = back_part(*tables, adjacency, back)
    input_grad = finish(picks, spread, returned, partial_grad)
    tiles, input_grad = lax.optimization_barrier((tiles, input_grad))
    weight_grad, bias_grad = join(tiles, lax.ppermute(tiles[:, 0:16], "core", swap))
    return (output, input_grad, weight_grad, bias_grad.reshape(F))


def solution(mesh):
    wide, narrow = mesh.devices.shape
    mesh = jax.sharding.Mesh(mesh.devices.reshape(wide // 2, 2, narrow), AXES)
    placed = (
        P(AXES, None),
        P(AXES, None, None),
        P(AXES, None),
        P(AXES, None),
        P(AXES),
        P(AXES),
        P(AXES, None, None),
        P(),
        P(),
        P(AXES, None),
    )
    return jax.shard_map(
        local,
        mesh=mesh,
        in_specs=placed,
        out_specs=(P(AXES, None), P(AXES, None), P(), P()),
        check_vma=False,
    )
```

```python
import math

import jax
import jax.numpy as jnp
from jax import lax
from jax.experimental import pallas as pl
from jax.experimental.pallas import tpu as pltpu
from jax.sharding import PartitionSpec as P

F = 512
BS = 128
NODES = 4096
HALO = 256
RB = 32
ECB = 40
BLK = 96
HALF = 2048
GROUP = 8
EARLY = 2
LAST = 127
DEVICES = 128
PEERS = 64
UNROLL = 16
FEW = 8
BF = jnp.bfloat16
F32 = jnp.float32
VMEM_BYTES = 24 * 1024 * 1024
VMEM_OWN = 24 * 1024 * 1024
VMEM_DENSE = 26 * 1024 * 1024
VMEM_BACK = 20 * 1024 * 1024
VMEM_FINISH = 8 * 1024 * 1024
WIDE = ("far", "core")
AXES = ("far", "core", "narrow")
CHIPS = ("far", "narrow")
SIDES = (WIDE, "narrow")


SMEM = pl.BlockSpec(memory_space=pltpu.SMEM)
VMEM = pl.BlockSpec(memory_space=pltpu.VMEM)
HBM = pl.BlockSpec(memory_space=pl.ANY)


def cost(us):
    return pl.CostEstimate(flops=int(us * 1e9), bytes_accessed=int(us * 3e6), transcendentals=0)


def held(x):
    return pltpu.with_memory_space_constraint(x, pltpu.VMEM)


def in_hbm(x):
    return pltpu.with_memory_space_constraint(x, pltpu.HBM)


def flips():
    return 1 - lax.axis_index("core"), 1 - (lax.axis_index("narrow") & 1)


def pick_row(picks, k, flip):
    return picks[pl.ds((k & 2) + ((k & 1) ^ flip[k // 2]), 1), :]


def pack_kernel(picks, feats_in, out0, out1, out2, out3, onehot, feats, sem):
    outs = (out0, out1, out2, out3)
    load = pltpu.make_async_copy(feats_in.at[pl.ds(0, HALF)], feats, sem.at[0])
    load.start()
    lane = lax.broadcasted_iota(jnp.int32, (BS, BS), 1)

    flip = flips()

    def build(k):
        line = pick_row(picks, k, flip)
        for h in range(2):
            row = line[:, h * BS : (h + 1) * BS]
            t = jnp.transpose(jnp.broadcast_to(row.astype(F32), (BS, BS))).astype(jnp.int32)
            for c in range(HALF // BS):
                hit = jnp.where(t == lane + c * BS, F32(1.0), F32(0.0)).astype(BF)
                onehot[k * HALO + h * BS : k * HALO + (h + 1) * BS, c * BS : (c + 1) * BS] = hit

    build(0)
    build(1)
    load.wait()
    for k in range(4):
        if k >= 2:
            build(k)
        outs[k][...] = jnp.dot(onehot[k * HALO : (k + 1) * HALO, :], feats[...], preferred_element_type=F32).astype(BF)


def pack(picks, features):
    return pl.pallas_call(
        pack_kernel,
        in_specs=[VMEM, HBM],
        out_specs=[VMEM] * 4,
        out_shape=[jax.ShapeDtypeStruct((HALO, F), BF)] * 4,
        scratch_shapes=[
            pltpu.VMEM((4 * HALO, HALF), BF),
            pltpu.VMEM((HALF, F), BF),
            pltpu.SemaphoreType.DMA((1,)),
        ],
        compiler_params=pltpu.CompilerParams(vmem_limit_bytes=VMEM_BYTES),
        cost_estimate=cost(3),
        name="pack",
    )(picks, in_hbm(features))


def block(ref, i):
    return ref[pl.ds(pl.multiple_of(i * BS, BS), BS), :]


def tail_mask(ref, start, alive):
    @pl.loop(start, RB)
    def _(r):
        at = pl.ds(pl.multiple_of(r * BS, BS), BS)
        line = lax.broadcasted_iota(jnp.int32, (BS, F), 0) + r * BS
        ref[at, :] = jnp.where(line < alive, ref[at, :].astype(F32), F32(0.0)).astype(BF)


def zero_blocks(ref, count):
    @pl.loop(0, count)
    def _(r):
        ref[pl.ds(pl.multiple_of(r * BS, BS), BS), :] = jnp.zeros((BS, F), F32)


def slot_lists(table, few, order, flag, rows, cols, live):
    flip = flips()
    for r in range(RB):
        flag[r] = jnp.int32(0)

    def step(b, sizes):
        n, m = sizes
        r, c = rows[0, b], cols[0, b]
        turn = jnp.where(c < RB, 0, jnp.where(c < RB + 4, flip[0], flip[1]) * 2)
        code = b + (r << 8) + ((c ^ turn) << 16)
        alive = (b < live).astype(jnp.int32)
        far = (c >= RB).astype(jnp.int32) * alive
        table[n] = code
        few[m] = code
        flag[r] = flag[r] | far
        return n + alive - far, m + far

    n, m = lax.fori_loop(0, BLK, step, (jnp.int32(0), jnp.int32(0)), unroll=4)
    for u in range(UNROLL):
        table[n + u] = jnp.int32((RB << 8) + (RB << 16))
    for u in range(FEW):
        few[m + u] = jnp.int32((RB << 8) + (ECB << 16))
    table[LAST] = (n + UNROLL - 1) // UNROLL
    few[LAST] = (m + FEW - 1) // FEW
    at = jnp.int32(0)
    for r in range(RB):
        order[at] = jnp.int32(r)
        at = at + 1 - flag[r]
    order[LAST] = jnp.minimum(at // GROUP, EARLY)
    for r in range(RB):
        order[at] = jnp.int32(r)
        at = at + flag[r]


def unpack(code):
    return code & 255, (code >> 8) & 255, code >> 16


def group_blocks(order, i):
    return [order[i * GROUP + j] for j in range(GROUP)]


def dense_group(ids, alive, acc, weight, bias, grads, outbuf, back, wacc, bacc, output, back_out, osems):
    ats = [pl.ds(pl.multiple_of(r * BS, BS), BS) for r in ids]
    agg = jnp.concatenate([acc[at, :].astype(BF) for at in ats], 0)
    pre = jnp.dot(agg, weight[...], preferred_element_type=F32) + bias[...]
    sig = jax.nn.sigmoid(pre)
    out = pre * sig
    slope = sig * (1.0 + pre * (1.0 - sig))
    dpres = []
    for j, (r, at) in enumerate(zip(ids, ats)):
        part = slice(j * BS, (j + 1) * BS)
        keep = lax.broadcasted_iota(jnp.int32, (BS, F), 0) + r * BS < alive
        outbuf[at, :] = jnp.where(keep, out[part], F32(0.0)).astype(BF)
        dpres.append(jnp.where(keep, grads[at, :].astype(F32) * slope[part], F32(0.0)).astype(BF))
    dpre = jnp.concatenate(dpres, 0)
    bacc[...] += jnp.sum(dpre.astype(F32).reshape(GROUP * BS // 8, 8, F), 0)
    wacc[...] += lax.dot_general(agg, dpre, (((0,), (0,)), ((), ())), preferred_element_type=F32)
    got = lax.dot_general(dpre, weight[...], (((1,), (1,)), ((), ())), preferred_element_type=F32).astype(BF)
    for j, (r, at) in enumerate(zip(ids, ats)):
        back[at, :] = got[j * BS : (j + 1) * BS]
    for r, at in zip(ids, ats):
        pltpu.make_async_copy(outbuf.at[at], output.at[at], osems.at[r]).start()
        pltpu.make_async_copy(back.at[at], back_out.at[at], osems.at[RB + r]).start()


def wait_group(ids, outbuf, back, output, back_out, osems):
    for r in ids:
        at = pl.ds(pl.multiple_of(r * BS, BS), BS)
        pltpu.make_async_copy(outbuf.at[at], output.at[at], osems.at[r]).wait()
        pltpu.make_async_copy(back.at[at], back_out.at[at], osems.at[RB + r]).wait()


def own_kernel(
    rows, cols, count, nodes, feats, adj_in, weight, bias, grads_in,
    acc, adj, wacc, bacc, output, back_out, order, few_table, table,
    ext, grads, outbuf, back, flag, sems, osems,
):
    alive = nodes[0]
    loads = [
        pltpu.make_async_copy(adj_in, adj, sems.at[0]),
        pltpu.make_async_copy(feats, ext.at[pl.ds(0, NODES)], sems.at[1]),
    ]
    late = pltpu.make_async_copy(grads_in, grads, sems.at[2])
    for c in loads:
        c.start()
    late.start()
    zero_blocks(acc, RB + 1)
    wacc[...] = jnp.zeros_like(wacc)
    bacc[...] = jnp.zeros_like(bacc)
    slot_lists(table, few_table, order, flag, rows, cols, count[0])
    groups, early = table[LAST], order[LAST]
    for c in loads:
        c.wait()
    tail_mask(ext, alive // BS, alive)

    @pl.loop(0, groups)
    def _(i):
        prods, targets = [], []
        for u in range(UNROLL):
            b, r, c = unpack(table[i * UNROLL + u])
            prods.append(jnp.dot(adj[b], block(ext, c), preferred_element_type=F32))
            targets.append(r)
        for prod, r in zip(prods, targets):
            at = pl.ds(pl.multiple_of(r * BS, BS), BS)
            acc[at, :] += prod

    late.wait()

    @pl.loop(0, early)
    def _(i):
        ids = group_blocks(order, i)
        dense_group(ids, alive, acc, weight, bias, grads, outbuf, back, wacc, bacc, output, back_out, osems)

    @pl.loop(0, early)
    def _(i):
        wait_group(group_blocks(order, i), outbuf, back, output, back_out, osems)


def own_part(rows, cols, count, nodes, features, adjacency, weight, bias, out_grad):
    return pl.pallas_call(
        own_kernel,
        in_specs=[SMEM] * 4 + [HBM] * 2 + [VMEM] * 2 + [HBM],
        out_specs=[VMEM] * 4 + [HBM] * 2 + [SMEM] * 3,
        out_shape=[
            pltpu.VMEM(((RB + 1) * BS, F), F32),
            pltpu.VMEM((BLK, BS, BS), BF),
            pltpu.VMEM((F, F), F32),
            pltpu.VMEM((8, F), F32),
            pltpu.HBM((NODES, F), BF),
            pltpu.HBM((NODES, F), BF),
            jax.ShapeDtypeStruct((128,), jnp.int32),
            jax.ShapeDtypeStruct((128,), jnp.int32),
            jax.ShapeDtypeStruct((128,), jnp.int32),
        ],
        scratch_shapes=[
            pltpu.VMEM(((RB + 1) * BS, F), BF),
            pltpu.VMEM((NODES, F), BF),
            pltpu.VMEM((NODES, F), BF),
            pltpu.VMEM((NODES, F), BF),
            pltpu.SMEM((RB,), jnp.int32),
            pltpu.SemaphoreType.DMA((3,)),
            pltpu.SemaphoreType.DMA((2 * RB,)),
        ],
        compiler_params=pltpu.CompilerParams(vmem_limit_bytes=VMEM_OWN),
        cost_estimate=cost(13),
        name="own_part",
    )(rows, cols, count, nodes, in_hbm(features), in_hbm(adjacency), weight, bias, in_hbm(out_grad))


def dense_kernel(
    nodes, order, table, acc_in, adj, wacc_in, bacc_in, h0, h1, h2, h3, weight, bias, grads_in, output_in, back_in,
    acc, output, back_out, ret0, ret1, ret2, ret3, mine, give, lines_out,
    back, received, spread, grads, outbuf, wacc, bacc, gsem, osems,
):
    alive = nodes[0]
    late = pltpu.make_async_copy(grads_in, grads, gsem.at[0])
    late.start()
    early = order[LAST]
    groups = table[LAST]
    zero_blocks(spread, ECB - RB + 1)
    wacc[...] = wacc_in[...]
    bacc[...] = bacc_in[...]
    for k, h in enumerate((h0, h1, h2, h3)):
        received[pl.ds(k * HALO, HALO), :] = h[...]

    @pl.loop(0, groups)
    def _(i):
        prods, targets = [], []
        for u in range(FEW):
            b, r, c = unpack(table[i * FEW + u])
            prods.append(jnp.dot(adj[b], block(received, c - RB), preferred_element_type=F32))
            targets.append(r)
        for prod, r in zip(prods, targets):
            at = pl.ds(pl.multiple_of(r * BS, BS), BS)
            acc[at, :] += prod

    late.wait()

    @pl.loop(early, RB // GROUP)
    def _(i):
        ids = group_blocks(order, i)
        dense_group(ids, alive, acc, weight, bias, grads, outbuf, back, wacc, bacc, output, back_out, osems)

    core = lax.axis_index("core")
    for out, half, kind in ((mine, core, F32), (give, 1 - core, BF)):
        for p in range(PEERS):
            for t in range(2):
                a, c = p // 2, p % 2 * 2 + t
                tile = wacc[pl.ds(pl.multiple_of(half * (F // 2) + a * 8, 8), 8), c * BS : (c + 1) * BS]
                out[p, 8 * t : 8 * t + 8, :] = tile.astype(kind)
    total = jnp.sum(bacc[...], 0, keepdims=True)
    high = total.astype(BF).astype(F32)
    low = total - high
    lines = jnp.concatenate(
        [high[:, c * BS : (c + 1) * BS] for c in range(4)] + [low[:, c * BS : (c + 1) * BS] for c in range(4)], 0
    ).astype(BF)
    lines_out[...] = lines
    give[PEERS] = jnp.concatenate([lines, lines], 0)

    @pl.loop(0, groups)
    def _(i):
        prods, targets = [], []
        for u in range(FEW):
            b, r, c = unpack(table[i * FEW + u])
            r = jnp.where(r < RB, r, 0)
            prods.append(
                lax.dot_general(adj[b], block(back, r), (((0,), (0,)), ((), ())), preferred_element_type=F32)
            )
            targets.append(c - RB)
        for prod, c in zip(prods, targets):
            at = pl.ds(pl.multiple_of(c * BS, BS), BS)
            spread[at, :] += prod

    for k, ret in enumerate((ret0, ret1, ret2, ret3)):
        ret[...] = spread[k * HALO : (k + 1) * HALO, :].astype(BF)

    @pl.loop(early, RB // GROUP)
    def _(i):
        wait_group(group_blocks(order, i), outbuf, back, output, back_out, osems)


def dense_part(nodes, order, table, acc, adj, wacc, bacc, halos, weight, bias, out_grad, output, back):
    return pl.pallas_call(
        dense_kernel,
        in_specs=[SMEM] * 3 + [VMEM] * 10 + [HBM] * 3,
        out_specs=[VMEM, HBM, HBM] + [VMEM] * 7,
        out_shape=[
            pltpu.VMEM(((RB + 1) * BS, F), F32),
            pltpu.HBM((NODES, F), BF),
            pltpu.HBM((NODES, F), BF),
        ]
        + [jax.ShapeDtypeStruct((HALO, F), BF)] * 4
        + [
            jax.ShapeDtypeStruct((PEERS, 16, BS), F32),
            jax.ShapeDtypeStruct((PEERS + 1, 16, BS), BF),
            jax.ShapeDtypeStruct((8, BS), BF),
        ],
        input_output_aliases={3: 0, 14: 1, 15: 2},
        scratch_shapes=[
            pltpu.VMEM((NODES, F), BF),
            pltpu.VMEM(((ECB - RB + 1) * BS, F), BF),
            pltpu.VMEM(((ECB - RB + 1) * BS, F), F32),
            pltpu.VMEM((NODES, F), BF),
            pltpu.VMEM((NODES, F), BF),
            pltpu.VMEM((F, F), F32),
            pltpu.VMEM((8, F), F32),
            pltpu.SemaphoreType.DMA((1,)),
            pltpu.SemaphoreType.DMA((2 * RB,)),
        ],
        compiler_params=pltpu.CompilerParams(vmem_limit_bytes=VMEM_DENSE),
        cost_estimate=cost(10),
        name="dense_part",
    )(
        nodes, order, table, held(acc), held(adj), held(wacc), held(bacc), *halos,
        weight, bias, in_hbm(out_grad), in_hbm(output), in_hbm(back),
    )[1:]


def back_kernel(
    nodes, table, adj_in, back_in, spread, input_grad, adj, back, outbuf, sems
):
    alive = nodes[0]
    loads = [
        pltpu.make_async_copy(adj_in, adj, sems.at[1]),
        pltpu.make_async_copy(back_in, back.at[pl.ds(0, NODES)], sems.at[2]),
    ]
    for c in loads:
        c.start()
    zero_blocks(spread, RB + 1)
    groups = table[LAST]
    for c in loads:
        c.wait()

    @pl.loop(0, groups)
    def _(i):
        prods, targets = [], []
        for u in range(UNROLL):
            b, r, c = unpack(table[i * UNROLL + u])
            prods.append(
                lax.dot_general(adj[b], block(back, r), (((0,), (0,)), ((), ())), preferred_element_type=F32)
            )
            targets.append(c)
        for prod, c in zip(prods, targets):
            at = pl.ds(pl.multiple_of(c * BS, BS), BS)
            spread[at, :] += prod

    @pl.loop(HALF // BS, RB)
    def _(r):
        at = pl.ds(pl.multiple_of(r * BS, BS), BS)
        to = pl.ds(pl.multiple_of(r * BS - HALF, BS), BS)
        line = lax.broadcasted_iota(jnp.int32, (BS, F), 0) + r * BS
        outbuf[to, :] = jnp.where(line < alive, spread[at, :], F32(0.0)).astype(BF)

    top = pltpu.make_async_copy(outbuf, input_grad.at[pl.ds(HALF, HALF)], sems.at[0])
    top.start()
    top.wait()


def back_part(nodes, table, adj, back):
    return pl.pallas_call(
        back_kernel,
        in_specs=[SMEM] * 2 + [HBM] * 2,
        out_specs=[VMEM, HBM],
        out_shape=[pltpu.VMEM(((RB + 1) * BS, F), F32), jax.ShapeDtypeStruct((NODES, F), BF)],
        scratch_shapes=[
            pltpu.VMEM((BLK, BS, BS), BF),
            pltpu.VMEM(((RB + 1) * BS, F), BF),
            pltpu.VMEM((HALF, F), BF),
            pltpu.SemaphoreType.DMA((3,)),
        ],
        compiler_params=pltpu.CompilerParams(vmem_limit_bytes=VMEM_BACK),
        cost_estimate=cost(9),
        name="back_part",
    )(nodes, table, in_hbm(adj), in_hbm(back))


def finish_kernel(picks, spread, r0, r1, r2, r3, partial, input_grad, outbuf, sems):
    line = lax.broadcasted_iota(jnp.int32, (HALO, HALO), 0)
    flip = flips()
    lines = [pick_row(picks, k, flip) for k in range(4)]

    @pl.loop(0, HALF // HALO)
    def _(i):
        at = pl.ds(pl.multiple_of(i * HALO, HALO), HALO)
        got = spread[at, :]
        for k, r in enumerate((r0, r1, r2, r3)):
            hit = jnp.where(line + i * HALO == lines[k], F32(1.0), F32(0.0)).astype(BF)
            got = got + jnp.dot(hit, r[...], preferred_element_type=F32)
        outbuf[at, :] = got.astype(BF)
        pltpu.make_async_copy(outbuf.at[at], input_grad.at[at], sems.at[0]).start()

    pltpu.make_async_copy(outbuf, input_grad.at[pl.ds(0, HALF)], sems.at[0]).wait()


def finish(picks, spread, returned, input_grad):
    return pl.pallas_call(
        finish_kernel,
        in_specs=[VMEM] * 6 + [HBM],
        out_specs=HBM,
        out_shape=jax.ShapeDtypeStruct((NODES, F), BF),
        input_output_aliases={6: 0},
        scratch_shapes=[pltpu.VMEM((HALF, F), BF), pltpu.SemaphoreType.DMA((1,))],
        compiler_params=pltpu.CompilerParams(vmem_limit_bytes=VMEM_FINISH),
        cost_estimate=cost(4),
        name="finish",
    )(picks, held(spread), *returned, input_grad)


def pair_kernel(mine, given, lines, pair, both_lines):
    pair[...] = (mine[...] + given[0:PEERS].astype(F32)).astype(BF)
    near, far = lines[...].astype(F32), given[PEERS, 0:8, :].astype(F32)
    both = near[0:4] + near[4:8] + (far[0:4] + far[4:8])
    high = both.astype(BF).astype(F32)
    both_lines[...] = jnp.concatenate([high, both - high], 0).astype(BF)


def pair_sum(mine, given, lines):
    return pl.pallas_call(
        pair_kernel,
        in_specs=[VMEM] * 3,
        out_specs=[VMEM] * 2,
        out_shape=[jax.ShapeDtypeStruct((PEERS, 16, BS), BF), jax.ShapeDtypeStruct((8, BS), BF)],
        compiler_params=pltpu.CompilerParams(vmem_limit_bytes=VMEM_FINISH),
        cost_estimate=cost(1),
        name="pair_sum",
    )(mine, given, lines)


def join_kernel(tiles, other, weight_grad, bias_grad):
    core = lax.axis_index("core")
    for half, src in ((core, tiles), (1 - core, other)):
        for p in range(PEERS):
            for t in range(2):
                a, c = p // 2, p % 2 * 2 + t
                at = pl.ds(pl.multiple_of(half * (F // 2) + a * 8, 8), 8)
                weight_grad[at, c * BS : (c + 1) * BS] = src[p, 8 * t : 8 * t + 8, :].astype(F32)
    sums = jnp.sum(tiles[:, 16:24, :].astype(F32), 0)
    bias_grad[...] = (sums[0:4] + sums[4:8]) * (1.0 / math.sqrt(NODES * DEVICES))


def join(tiles, other):
    return pl.pallas_call(
        join_kernel,
        in_specs=[VMEM] * 2,
        out_specs=[VMEM] * 2,
        out_shape=[jax.ShapeDtypeStruct((F, F), F32), jax.ShapeDtypeStruct((F // BS, BS), F32)],
        compiler_params=pltpu.CompilerParams(vmem_limit_bytes=VMEM_FINISH),
        cost_estimate=cost(1),
        name="join",
    )(tiles, other)


def exchange(parts):
    got = [None] * 4
    for k in (1, 3, 0, 2):
        axis = SIDES[k // 2]
        pairs = [p for i in range(k % 2, lax.axis_size(axis) - 1, 2) for p in ((i, i + 1), (i + 1, i))]
        got[k] = lax.ppermute(parts[k], axis, pairs)
    return got


def local(features, adjacency, block_rows, block_cols, block_count, node_count, halo_index, weight, bias, out_grad):
    picks = halo_index.reshape(4, HALO)
    tables = (block_rows, block_cols, block_count, node_count)
    packed = pack(picks, features)
    packed, adjacency = lax.optimization_barrier((packed, adjacency))
    bias = bias.reshape(1, F)
    acc, adj, wacc, bacc, output, back, order, few, table = own_part(*tables, features, adjacency, weight, bias, out_grad)
    halos = exchange(packed)
    output, back, r0, r1, r2, r3, mine, give, lines = dense_part(
        node_count, order, few, acc, adj, wacc, bacc, halos, weight, bias, out_grad, output, back
    )
    scale = 1.0 / math.sqrt(NODES * DEVICES)
    swap = [(0, 1), (1, 0)]
    pair, lines = pair_sum(mine, lax.ppermute(give, "core", swap), lines)
    pair, r0, r1, r2, r3 = lax.optimization_barrier((pair, r0, r1, r2, r3))
    returned = exchange((r0, r1, r2, r3))
    gathered = lax.all_to_all(pair, CHIPS, 0, 0, tiled=True).astype(F32)
    share = (jnp.sum(gathered, 0) * scale).astype(BF)
    tiles = jnp.broadcast_to(jnp.concatenate([share, lines], 0)[None], (PEERS, 24, BS))
    tiles, adjacency = lax.optimization_barrier((tiles, adjacency))
    tiles = lax.all_to_all(tiles, CHIPS, 0, 0, tiled=True)
    spread, partial_grad = back_part(node_count, table, adjacency, back)
    input_grad = finish(picks, spread, returned, partial_grad)
    tiles, input_grad = lax.optimization_barrier((tiles, input_grad))
    weight_grad, bias_grad = join(tiles, lax.ppermute(tiles[:, 0:16], "core", swap))
    return (output, input_grad, weight_grad, bias_grad.reshape(F))


def solution(mesh):
    wide, narrow = mesh.devices.shape
    mesh = jax.sharding.Mesh(mesh.devices.reshape(wide // 2, 2, narrow), AXES)
    placed = (
        P(AXES, None),
        P(AXES, None, None),
        P(AXES, None),
        P(AXES, None),
        P(AXES),
        P(AXES),
        P(AXES, None, None),
        P(),
        P(),
        P(AXES, None),
    )
    return jax.shard_map(
        local,
        mesh=mesh,
        in_specs=placed,
        out_specs=(P(AXES, None), P(AXES, None), P(), P()),
        check_vma=False,
    )
```

```python
import math

import jax
import jax.numpy as jnp
from jax import lax
from jax.experimental import pallas as pl
from jax.experimental.pallas import tpu as pltpu
from jax.sharding import PartitionSpec as P

F = 512
BS = 128
NODES = 4096
HALO = 256
RB = 32
ECB = 40
BLK = 96
HALF = 2048
GROUP = 8
EARLY = 2
LAST = 127
DEVICES = 128
PEERS = 64
UNROLL = 20
FEW = 8
BF = jnp.bfloat16
F32 = jnp.float32
VMEM_BYTES = 24 * 1024 * 1024
VMEM_OWN = 24 * 1024 * 1024
VMEM_DENSE = 26 * 1024 * 1024
VMEM_BACK = 20 * 1024 * 1024
VMEM_FINISH = 8 * 1024 * 1024
WIDE = ("far", "core")
AXES = ("far", "core", "narrow")
CHIPS = ("far", "narrow")
SIDES = (WIDE, "narrow")


SMEM = pl.BlockSpec(memory_space=pltpu.SMEM)
VMEM = pl.BlockSpec(memory_space=pltpu.VMEM)
HBM = pl.BlockSpec(memory_space=pl.ANY)


def cost(us):
    return pl.CostEstimate(flops=int(us * 1e9), bytes_accessed=int(us * 3e6), transcendentals=0)


def held(x):
    return pltpu.with_memory_space_constraint(x, pltpu.VMEM)


def in_hbm(x):
    return pltpu.with_memory_space_constraint(x, pltpu.HBM)


def flips():
    return 1 - lax.axis_index("core"), 1 - (lax.axis_index("narrow") & 1)


def pick_row(picks, k, flip):
    return picks[pl.ds((k & 2) + ((k & 1) ^ flip[k // 2]), 1), :]


def pack_kernel(picks, feats_in, out0, out1, out2, out3, onehot, feats, sem):
    outs = (out0, out1, out2, out3)
    load = pltpu.make_async_copy(feats_in.at[pl.ds(0, HALF)], feats, sem.at[0])
    load.start()
    lane = lax.broadcasted_iota(jnp.int32, (BS, BS), 1)

    flip = flips()

    def build(k):
        line = pick_row(picks, k, flip)
        for h in range(2):
            row = line[:, h * BS : (h + 1) * BS]
            t = jnp.transpose(jnp.broadcast_to(row.astype(F32), (BS, BS))).astype(jnp.int32)
            for c in range(HALF // BS):
                hit = jnp.where(t == lane + c * BS, F32(1.0), F32(0.0)).astype(BF)
                onehot[k * HALO + h * BS : k * HALO + (h + 1) * BS, c * BS : (c + 1) * BS] = hit

    build(0)
    build(1)
    load.wait()
    for k in range(4):
        if k >= 2:
            build(k)
        outs[k][...] = jnp.dot(onehot[k * HALO : (k + 1) * HALO, :], feats[...], preferred_element_type=F32).astype(BF)


def pack(picks, features):
    return pl.pallas_call(
        pack_kernel,
        in_specs=[VMEM, HBM],
        out_specs=[VMEM] * 4,
        out_shape=[jax.ShapeDtypeStruct((HALO, F), BF)] * 4,
        scratch_shapes=[
            pltpu.VMEM((4 * HALO, HALF), BF),
            pltpu.VMEM((HALF, F), BF),
            pltpu.SemaphoreType.DMA((1,)),
        ],
        compiler_params=pltpu.CompilerParams(vmem_limit_bytes=VMEM_BYTES),
        cost_estimate=cost(3),
        name="pack",
    )(picks, in_hbm(features))


def block(ref, i):
    return ref[pl.ds(pl.multiple_of(i * BS, BS), BS), :]


def tail_mask(ref, start, alive):
    @pl.loop(start, RB)
    def _(r):
        at = pl.ds(pl.multiple_of(r * BS, BS), BS)
        line = lax.broadcasted_iota(jnp.int32, (BS, F), 0) + r * BS
        ref[at, :] = jnp.where(line < alive, ref[at, :].astype(F32), F32(0.0)).astype(BF)


def zero_blocks(ref, count):
    @pl.loop(0, count)
    def _(r):
        ref[pl.ds(pl.multiple_of(r * BS, BS), BS), :] = jnp.zeros((BS, F), F32)


def slot_lists(table, few, order, flag, rows, cols, live):
    flip = flips()
    for r in range(RB):
        flag[r] = jnp.int32(0)

    def step(b, sizes):
        n, m = sizes
        r, c = rows[0, b], cols[0, b]
        turn = jnp.where(c < RB, 0, jnp.where(c < RB + 4, flip[0], flip[1]) * 2)
        code = b + (r << 8) + ((c ^ turn) << 16)
        alive = (b < live).astype(jnp.int32)
        far = (c >= RB).astype(jnp.int32) * alive
        table[n] = code
        few[m] = code
        flag[r] = flag[r] | far
        return n + alive - far, m + far

    n, m = lax.fori_loop(0, BLK, step, (jnp.int32(0), jnp.int32(0)), unroll=4)
    for u in range(UNROLL):
        table[n + u] = jnp.int32((RB << 8) + (RB << 16))
    for u in range(FEW):
        few[m + u] = jnp.int32((RB << 8) + (ECB << 16))
    table[LAST] = (n + UNROLL - 1) // UNROLL
    few[LAST] = (m + FEW - 1) // FEW
    at = jnp.int32(0)
    for r in range(RB):
        order[at] = jnp.int32(r)
        at = at + 1 - flag[r]
    order[LAST] = jnp.minimum(at // GROUP, EARLY)
    for r in range(RB):
        order[at] = jnp.int32(r)
        at = at + flag[r]


def unpack(code):
    return code & 255, (code >> 8) & 255, code >> 16


def group_blocks(order, i):
    return [order[i * GROUP + j] for j in range(GROUP)]


def dense_group(ids, alive, acc, weight, bias, grads, outbuf, back, wacc, bacc, output, back_out, osems):
    ats = [pl.ds(pl.multiple_of(r * BS, BS), BS) for r in ids]
    agg = jnp.concatenate([acc[at, :].astype(BF) for at in ats], 0)
    pre = jnp.dot(agg, weight[...], preferred_element_type=F32) + bias[...]
    sig = jax.nn.sigmoid(pre)
    out = pre * sig
    slope = sig * (1.0 + pre * (1.0 - sig))
    dpres = []
    for j, (r, at) in enumerate(zip(ids, ats)):
        part = slice(j * BS, (j + 1) * BS)
        keep = lax.broadcasted_iota(jnp.int32, (BS, F), 0) + r * BS < alive
        outbuf[at, :] = jnp.where(keep, out[part], F32(0.0)).astype(BF)
        dpres.append(jnp.where(keep, grads[at, :].astype(F32) * slope[part], F32(0.0)).astype(BF))
    dpre = jnp.concatenate(dpres, 0)
    bacc[...] += jnp.sum(dpre.astype(F32).reshape(GROUP * BS // 8, 8, F), 0)
    wacc[...] += lax.dot_general(agg, dpre, (((0,), (0,)), ((), ())), preferred_element_type=F32)
    got = lax.dot_general(dpre, weight[...], (((1,), (1,)), ((), ())), preferred_element_type=F32).astype(BF)
    for j, (r, at) in enumerate(zip(ids, ats)):
        back[at, :] = got[j * BS : (j + 1) * BS]
    for r, at in zip(ids, ats):
        pltpu.make_async_copy(outbuf.at[at], output.at[at], osems.at[r]).start()
        pltpu.make_async_copy(back.at[at], back_out.at[at], osems.at[RB + r]).start()


def wait_group(ids, outbuf, back, output, back_out, osems):
    for r in ids:
        at = pl.ds(pl.multiple_of(r * BS, BS), BS)
        pltpu.make_async_copy(outbuf.at[at], output.at[at], osems.at[r]).wait()
        pltpu.make_async_copy(back.at[at], back_out.at[at], osems.at[RB + r]).wait()


def own_kernel(
    rows, cols, count, nodes, feats, adj_in, weight, bias, grads_in,
    acc, adj, wacc, bacc, output, back_out, order, few_table, table,
    ext, grads, outbuf, back, flag, sems, osems,
):
    alive = nodes[0]
    loads = [
        pltpu.make_async_copy(adj_in, adj, sems.at[0]),
        pltpu.make_async_copy(feats, ext.at[pl.ds(0, NODES)], sems.at[1]),
    ]
    late = pltpu.make_async_copy(grads_in, grads, sems.at[2])
    for c in loads:
        c.start()
    late.start()
    zero_blocks(acc, RB + 1)
    wacc[...] = jnp.zeros_like(wacc)
    bacc[...] = jnp.zeros_like(bacc)
    slot_lists(table, few_table, order, flag, rows, cols, count[0])
    groups, early = table[LAST], order[LAST]
    for c in loads:
        c.wait()
    tail_mask(ext, alive // BS, alive)

    @pl.loop(0, groups)
    def _(i):
        prods, targets = [], []
        for u in range(UNROLL):
            b, r, c = unpack(table[i * UNROLL + u])
            prods.append(jnp.dot(adj[b], block(ext, c), preferred_element_type=F32))
            targets.append(r)
        for prod, r in zip(prods, targets):
            at = pl.ds(pl.multiple_of(r * BS, BS), BS)
            acc[at, :] += prod

    late.wait()

    @pl.loop(0, early)
    def _(i):
        ids = group_blocks(order, i)
        dense_group(ids, alive, acc, weight, bias, grads, outbuf, back, wacc, bacc, output, back_out, osems)

    @pl.loop(0, early)
    def _(i):
        wait_group(group_blocks(order, i), outbuf, back, output, back_out, osems)


def own_part(rows, cols, count, nodes, features, adjacency, weight, bias, out_grad):
    return pl.pallas_call(
        own_kernel,
        in_specs=[SMEM] * 4 + [HBM] * 2 + [VMEM] * 2 + [HBM],
        out_specs=[VMEM] * 4 + [HBM] * 2 + [SMEM] * 3,
        out_shape=[
            pltpu.VMEM(((RB + 1) * BS, F), F32),
            pltpu.VMEM((BLK, BS, BS), BF),
            pltpu.VMEM((F, F), F32),
            pltpu.VMEM((8, F), F32),
            pltpu.HBM((NODES, F), BF),
            pltpu.HBM((NODES, F), BF),
            jax.ShapeDtypeStruct((128,), jnp.int32),
            jax.ShapeDtypeStruct((128,), jnp.int32),
            jax.ShapeDtypeStruct((128,), jnp.int32),
        ],
        scratch_shapes=[
            pltpu.VMEM(((RB + 1) * BS, F), BF),
            pltpu.VMEM((NODES, F), BF),
            pltpu.VMEM((NODES, F), BF),
            pltpu.VMEM((NODES, F), BF),
            pltpu.SMEM((RB,), jnp.int32),
            pltpu.SemaphoreType.DMA((3,)),
            pltpu.SemaphoreType.DMA((2 * RB,)),
        ],
        compiler_params=pltpu.CompilerParams(vmem_limit_bytes=VMEM_OWN),
        cost_estimate=cost(13),
        name="own_part",
    )(rows, cols, count, nodes, in_hbm(features), in_hbm(adjacency), weight, bias, in_hbm(out_grad))


def dense_kernel(
    nodes, order, table, acc_in, adj, wacc_in, bacc_in, h0, h1, h2, h3, weight, bias, grads_in, output_in, back_in,
    acc, output, back_out, ret0, ret1, ret2, ret3, mine, give, lines_out,
    back, received, spread, grads, outbuf, wacc, bacc, gsem, osems,
):
    alive = nodes[0]
    late = pltpu.make_async_copy(grads_in, grads, gsem.at[0])
    late.start()
    early = order[LAST]
    groups = table[LAST]
    zero_blocks(spread, ECB - RB + 1)
    wacc[...] = wacc_in[...]
    bacc[...] = bacc_in[...]
    for k, h in enumerate((h0, h1, h2, h3)):
        received[pl.ds(k * HALO, HALO), :] = h[...]

    @pl.loop(0, groups)
    def _(i):
        prods, targets = [], []
        for u in range(FEW):
            b, r, c = unpack(table[i * FEW + u])
            prods.append(jnp.dot(adj[b], block(received, c - RB), preferred_element_type=F32))
            targets.append(r)
        for prod, r in zip(prods, targets):
            at = pl.ds(pl.multiple_of(r * BS, BS), BS)
            acc[at, :] += prod

    late.wait()

    @pl.loop(early, RB // GROUP)
    def _(i):
        ids = group_blocks(order, i)
        dense_group(ids, alive, acc, weight, bias, grads, outbuf, back, wacc, bacc, output, back_out, osems)

    core = lax.axis_index("core")
    for out, half, kind in ((mine, core, F32), (give, 1 - core, BF)):
        for p in range(PEERS):
            for t in range(2):
                a, c = p // 2, p % 2 * 2 + t
                tile = wacc[pl.ds(pl.multiple_of(half * (F // 2) + a * 8, 8), 8), c * BS : (c + 1) * BS]
                out[p, 8 * t : 8 * t + 8, :] = tile.astype(kind)
    total = jnp.sum(bacc[...], 0, keepdims=True)
    high = total.astype(BF).astype(F32)
    low = total - high
    lines = jnp.concatenate(
        [high[:, c * BS : (c + 1) * BS] for c in range(4)] + [low[:, c * BS : (c + 1) * BS] for c in range(4)], 0
    ).astype(BF)
    lines_out[...] = lines
    give[PEERS] = jnp.concatenate([lines, lines], 0)

    @pl.loop(0, groups)
    def _(i):
        prods, targets = [], []
        for u in range(FEW):
            b, r, c = unpack(table[i * FEW + u])
            r = jnp.where(r < RB, r, 0)
            prods.append(
                lax.dot_general(adj[b], block(back, r), (((0,), (0,)), ((), ())), preferred_element_type=F32)
            )
            targets.append(c - RB)
        for prod, c in zip(prods, targets):
            at = pl.ds(pl.multiple_of(c * BS, BS), BS)
            spread[at, :] += prod

    for k, ret in enumerate((ret0, ret1, ret2, ret3)):
        ret[...] = spread[k * HALO : (k + 1) * HALO, :].astype(BF)

    @pl.loop(early, RB // GROUP)
    def _(i):
        wait_group(group_blocks(order, i), outbuf, back, output, back_out, osems)


def dense_part(nodes, order, table, acc, adj, wacc, bacc, halos, weight, bias, out_grad, output, back):
    return pl.pallas_call(
        dense_kernel,
        in_specs=[SMEM] * 3 + [VMEM] * 10 + [HBM] * 3,
        out_specs=[VMEM, HBM, HBM] + [VMEM] * 7,
        out_shape=[
            pltpu.VMEM(((RB + 1) * BS, F), F32),
            pltpu.HBM((NODES, F), BF),
            pltpu.HBM((NODES, F), BF),
        ]
        + [jax.ShapeDtypeStruct((HALO, F), BF)] * 4
        + [
            jax.ShapeDtypeStruct((PEERS, 16, BS), F32),
            jax.ShapeDtypeStruct((PEERS + 1, 16, BS), BF),
            jax.ShapeDtypeStruct((8, BS), BF),
        ],
        input_output_aliases={3: 0, 14: 1, 15: 2},
        scratch_shapes=[
            pltpu.VMEM((NODES, F), BF),
            pltpu.VMEM(((ECB - RB + 1) * BS, F), BF),
            pltpu.VMEM(((ECB - RB + 1) * BS, F), F32),
            pltpu.VMEM((NODES, F), BF),
            pltpu.VMEM((NODES, F), BF),
            pltpu.VMEM((F, F), F32),
            pltpu.VMEM((8, F), F32),
            pltpu.SemaphoreType.DMA((1,)),
            pltpu.SemaphoreType.DMA((2 * RB,)),
        ],
        compiler_params=pltpu.CompilerParams(vmem_limit_bytes=VMEM_DENSE),
        cost_estimate=cost(10),
        name="dense_part",
    )(
        nodes, order, table, held(acc), held(adj), held(wacc), held(bacc), *halos,
        weight, bias, in_hbm(out_grad), in_hbm(output), in_hbm(back),
    )[1:]


def back_kernel(
    nodes, table, adj_in, back_in, spread, input_grad, adj, back, outbuf, sems
):
    alive = nodes[0]
    loads = [
        pltpu.make_async_copy(adj_in, adj, sems.at[1]),
        pltpu.make_async_copy(back_in, back.at[pl.ds(0, NODES)], sems.at[2]),
    ]
    for c in loads:
        c.start()
    zero_blocks(spread, RB + 1)
    groups = table[LAST]
    for c in loads:
        c.wait()

    @pl.loop(0, groups)
    def _(i):
        prods, targets = [], []
        for u in range(UNROLL):
            b, r, c = unpack(table[i * UNROLL + u])
            prods.append(
                lax.dot_general(adj[b], block(back, r), (((0,), (0,)), ((), ())), preferred_element_type=F32)
            )
            targets.append(c)
        for prod, c in zip(prods, targets):
            at = pl.ds(pl.multiple_of(c * BS, BS), BS)
            spread[at, :] += prod

    @pl.loop(HALF // BS, RB)
    def _(r):
        at = pl.ds(pl.multiple_of(r * BS, BS), BS)
        to = pl.ds(pl.multiple_of(r * BS - HALF, BS), BS)
        line = lax.broadcasted_iota(jnp.int32, (BS, F), 0) + r * BS
        outbuf[to, :] = jnp.where(line < alive, spread[at, :], F32(0.0)).astype(BF)

    top = pltpu.make_async_copy(outbuf, input_grad.at[pl.ds(HALF, HALF)], sems.at[0])
    top.start()
    top.wait()


def back_part(nodes, table, adj, back):
    return pl.pallas_call(
        back_kernel,
        in_specs=[SMEM] * 2 + [HBM] * 2,
        out_specs=[VMEM, HBM],
        out_shape=[pltpu.VMEM(((RB + 1) * BS, F), F32), jax.ShapeDtypeStruct((NODES, F), BF)],
        scratch_shapes=[
            pltpu.VMEM((BLK, BS, BS), BF),
            pltpu.VMEM(((RB + 1) * BS, F), BF),
            pltpu.VMEM((HALF, F), BF),
            pltpu.SemaphoreType.DMA((3,)),
        ],
        compiler_params=pltpu.CompilerParams(vmem_limit_bytes=VMEM_BACK),
        cost_estimate=cost(9),
        name="back_part",
    )(nodes, table, in_hbm(adj), in_hbm(back))


def finish_kernel(picks, spread, r0, r1, r2, r3, partial, input_grad, outbuf, sems):
    line = lax.broadcasted_iota(jnp.int32, (HALO, HALO), 0)
    flip = flips()
    lines = [pick_row(picks, k, flip) for k in range(4)]

    @pl.loop(0, HALF // HALO)
    def _(i):
        at = pl.ds(pl.multiple_of(i * HALO, HALO), HALO)
        got = spread[at, :]
        for k, r in enumerate((r0, r1, r2, r3)):
            hit = jnp.where(line + i * HALO == lines[k], F32(1.0), F32(0.0)).astype(BF)
            got = got + jnp.dot(hit, r[...], preferred_element_type=F32)
        outbuf[at, :] = got.astype(BF)
        pltpu.make_async_copy(outbuf.at[at], input_grad.at[at], sems.at[0]).start()

    pltpu.make_async_copy(outbuf, input_grad.at[pl.ds(0, HALF)], sems.at[0]).wait()


def finish(picks, spread, returned, input_grad):
    return pl.pallas_call(
        finish_kernel,
        in_specs=[VMEM] * 6 + [HBM],
        out_specs=HBM,
        out_shape=jax.ShapeDtypeStruct((NODES, F), BF),
        input_output_aliases={6: 0},
        scratch_shapes=[pltpu.VMEM((HALF, F), BF), pltpu.SemaphoreType.DMA((1,))],
        compiler_params=pltpu.CompilerParams(vmem_limit_bytes=VMEM_FINISH),
        cost_estimate=cost(4),
        name="finish",
    )(picks, held(spread), *returned, input_grad)


def pair_kernel(mine, given, lines, pair, both_lines):
    pair[...] = (mine[...] + given[0:PEERS].astype(F32)).astype(BF)
    near, far = lines[...].astype(F32), given[PEERS, 0:8, :].astype(F32)
    both = near[0:4] + near[4:8] + (far[0:4] + far[4:8])
    high = both.astype(BF).astype(F32)
    both_lines[...] = jnp.concatenate([high, both - high], 0).astype(BF)


def pair_sum(mine, given, lines):
    return pl.pallas_call(
        pair_kernel,
        in_specs=[VMEM] * 3,
        out_specs=[VMEM] * 2,
        out_shape=[jax.ShapeDtypeStruct((PEERS, 16, BS), BF), jax.ShapeDtypeStruct((8, BS), BF)],
        compiler_params=pltpu.CompilerParams(vmem_limit_bytes=VMEM_FINISH),
        cost_estimate=cost(1),
        name="pair_sum",
    )(mine, given, lines)


def join_kernel(tiles, other, weight_grad, bias_grad):
    core = lax.axis_index("core")
    for half, src in ((core, tiles), (1 - core, other)):
        for p in range(PEERS):
            for t in range(2):
                a, c = p // 2, p % 2 * 2 + t
                at = pl.ds(pl.multiple_of(half * (F // 2) + a * 8, 8), 8)
                weight_grad[at, c * BS : (c + 1) * BS] = src[p, 8 * t : 8 * t + 8, :].astype(F32)
    sums = jnp.sum(tiles[:, 16:24, :].astype(F32), 0)
    bias_grad[...] = (sums[0:4] + sums[4:8]) * (1.0 / math.sqrt(NODES * DEVICES))


def join(tiles, other):
    return pl.pallas_call(
        join_kernel,
        in_specs=[VMEM] * 2,
        out_specs=[VMEM] * 2,
        out_shape=[jax.ShapeDtypeStruct((F, F), F32), jax.ShapeDtypeStruct((F // BS, BS), F32)],
        compiler_params=pltpu.CompilerParams(vmem_limit_bytes=VMEM_FINISH),
        cost_estimate=cost(1),
        name="join",
    )(tiles, other)


def exchange(parts):
    got = [None] * 4
    for k in (1, 3, 0, 2):
        axis = SIDES[k // 2]
        pairs = [p for i in range(k % 2, lax.axis_size(axis) - 1, 2) for p in ((i, i + 1), (i + 1, i))]
        got[k] = lax.ppermute(parts[k], axis, pairs)
    return got


def local(features, adjacency, block_rows, block_cols, block_count, node_count, halo_index, weight, bias, out_grad):
    picks = halo_index.reshape(4, HALO)
    tables = (block_rows, block_cols, block_count, node_count)
    packed = pack(picks, features)
    packed, adjacency = lax.optimization_barrier((packed, adjacency))
    bias = bias.reshape(1, F)
    acc, adj, wacc, bacc, output, back, order, few, table = own_part(*tables, features, adjacency, weight, bias, out_grad)
    halos = exchange(packed)
    output, back, r0, r1, r2, r3, mine, give, lines = dense_part(
        node_count, order, few, acc, adj, wacc, bacc, halos, weight, bias, out_grad, output, back
    )
    scale = 1.0 / math.sqrt(NODES * DEVICES)
    swap = [(0, 1), (1, 0)]
    pair, lines = pair_sum(mine, lax.ppermute(give, "core", swap), lines)
    pair, r0, r1, r2, r3 = lax.optimization_barrier((pair, r0, r1, r2, r3))
    returned = exchange((r0, r1, r2, r3))
    gathered = lax.all_to_all(pair, CHIPS, 0, 0, tiled=True).astype(F32)
    share = (jnp.sum(gathered, 0) * scale).astype(BF)
    tiles = jnp.broadcast_to(jnp.concatenate([share, lines], 0)[None], (PEERS, 24, BS))
    tiles, adjacency = lax.optimization_barrier((tiles, adjacency))
    tiles = lax.all_to_all(tiles, CHIPS, 0, 0, tiled=True)
    spread, partial_grad = back_part(node_count, table, adjacency, back)
    input_grad = finish(picks, spread, returned, partial_grad)
    tiles, input_grad = lax.optimization_barrier((tiles, input_grad))
    weight_grad, bias_grad = join(tiles, lax.ppermute(tiles[:, 0:16], "core", swap))
    return (output, input_grad, weight_grad, bias_grad.reshape(F))


def solution(mesh):
    wide, narrow = mesh.devices.shape
    mesh = jax.sharding.Mesh(mesh.devices.reshape(wide // 2, 2, narrow), AXES)
    placed = (
        P(AXES, None),
        P(AXES, None, None),
        P(AXES, None),
        P(AXES, None),
        P(AXES),
        P(AXES),
        P(AXES, None, None),
        P(),
        P(),
        P(AXES, None),
    )
    return jax.shard_map(
        local,
        mesh=mesh,
        in_specs=placed,
        out_specs=(P(AXES, None), P(AXES, None), P(), P()),
        check_vma=False,
    )
```
